32 devices in a mesh: gx: 4 (over x, core), gy: 8 (over z, y).
Axes of the slice: x: 2, y: 2, z: 4, core: 2. Of those that a mesh axis runs over, the one named last changes fastest.
Arguments:
- fine_atmospheric_values: float32 [4, 768, 768], P(None, 'gx', 'gy'), may hold values from -6 to 6
- fine_skin_heat: float32 [768, 768], P('gx', 'gy'), may hold values from -6 to 6
- coarse_lowest_values: bfloat16 [4, 1536, 3072], P(None, 'gx', 'gy'), may hold values from -6 to 6
- holder_flat: int32 [1], replicated, may hold values from 0 to 31
- corner_offset: int32 [2], replicated, may hold values from 0 to 264
- exchange_patch_holder: int32 [4608, 1], P(('gx', 'gy')), may hold values from 0 to 31; in each aligned block of 144 rows (0 to 143, 144 to 287, ...) at most 9 rows name the same one
- holder_patch_position: int32 [4608], P(('gx', 'gy')), may hold values from 0 to 31
- coarse_interface_exchange: float32 [4, 131072], P(None, ('gx', 'gy')), may hold values from -6 to 6
- marine_stratum_values: float32 [4, 41, 131072], P(None, None, ('gx', 'gy')), may hold values from -6 to 6
- diffusion_solver_operator: float32 [41, 41], replicated, may hold values from -0.3 to 1
Outputs:
- nest_next: float32 [4, 768, 768], P(None, 'gx', 'gy')
- refreshed_marine_values: float32 [4, 41, 131072], P(None, None, ('gx', 'gy'))
- fine_refreshed_skin_heat: float32 [768, 768], P('gx', 'gy')
The draws below stay inside these ranges and needn't reach their ends.
Inputs may be any that keep to these rules, and one draw needn't show every extreme that they name: `holder_flat`: index of the tile that holds the storm. `corner_offset`: the nest lies inside the owner tile. `exchange_patch_holder`: within the blocks of one device, no ocean owner is named more than 9 times.
All inputs are finite; a program needn't handle non-finite values.
Results may differ from the reference program's by a relative error of at most 0.0019.
Values may be sent and summed in bfloat16 or wider, within the bound.
A program may use at most 64 MiB of HBM per device.

```python
import math
import jax
import jax.numpy as jnp
import numpy as np
from jax import lax

FIELDS = 4
CHIP_FINE_EAST = 192
CHIP_FINE_NORTH = 96
PC = 384
EXCHANGE_PATCH = 128
MARINE_PATCHES = 32
LAYERS = 41
STEPS = 4
FINE_EASTWARD = 768
FINE_NORTHWARD = 768
NB = 144
CAP = 9
TOTB = 4608
OCEAN_CELLS = 131072
WINX = 120
WINY = 120
PARX = 1536
PARY = 3072
N_GX = 4
N_GY = 8
DEVICES = 32


def draw_diffusion_solver_operator(key, part):
    first_key, second_key = jax.random.split(jax.random.fold_in(key, 11))
    diagonal = jax.random.uniform(first_key, (LAYERS,), jnp.float32, 0.6, 1.0)
    spread = 0.06 * jax.random.normal(second_key, (LAYERS, LAYERS), jnp.float32)
    spread = jnp.clip(spread, -0.3, 0.3)
    identity = jnp.eye(LAYERS, dtype=jnp.float32)
    return identity * diagonal[None, :] + (1.0 - identity) * spread


def with_ends(values, own_key, least, largest):
    spot = [jax.random.randint(jax.random.fold_in(own_key, axis), (), 0, length) for axis, length in enumerate(values.shape)]
    widest = values.shape.index(max(values.shape))
    beside = spot[:widest] + [(spot[widest] + 1) % values.shape[widest]] + spot[widest + 1:]
    return values.at[tuple(spot)].set(least).at[tuple(beside)].set(largest)


def level_of(own_key, extent, shards, smallest, largest):
    level = 1.0
    for dim, shards_of in shards:
        heights = jax.random.uniform(jax.random.fold_in(jax.random.fold_in(own_key, 6), dim), (shards_of,), jnp.float32, smallest / len(shards), largest / len(shards))
        level = level * jnp.repeat(jnp.exp(heights), extent[dim] // shards_of).reshape((-1,) + (1,) * (len(extent) - 1 - dim))
    return level


def routed_block(rng, own, number, rows, amount, top, most, skew):
    ranking = jax.random.permutation(rng, amount)
    crowded, usual = portions_of(amount, rows * top, most, skew, True), portions_of(amount, rows * top, most, skew, False)
    places = jnp.arange(amount)

    def named(tallies, offset_by):
        used = int((tallies > 0).sum())
        fixed = max(1, used // 4)
        passed = fixed + (places - fixed + offset_by * (used - fixed)) % max(1, amount - fixed)
        return jnp.zeros((amount,), jnp.int32).at[ranking[jnp.where(places < fixed, places, passed)]].set(jnp.asarray(tallies, jnp.int32))

    tallies = jnp.where(number % 4 == 0, named(crowded, number // 4), named(usual, number - number // 4 - 1))
    mixed = jax.random.permutation(jax.random.fold_in(own, 3), amount)
    source_of, receiver = mixed[0:amount // 2 * 2:2], mixed[1:amount // 2 * 2:2]
    margin = jnp.minimum(tallies[source_of] - 1, most - tallies[receiver]) // 2
    margin = jnp.where((source_of == ranking[0]) | (receiver == ranking[0]) | (tallies[receiver] == 0), 0, jnp.maximum(margin, 0))
    passed = jax.random.randint(jax.random.fold_in(own, 4), (amount // 2,), 0, 1 << 20) % (margin + 1)
    tallies = tallies.at[source_of].add(-passed).at[receiver].add(passed)
    members = jnp.searchsorted(jnp.cumsum(tallies), jnp.arange(rows * top), side="right").astype(jnp.int32)
    grid = members.reshape(top, rows).T
    grid = grid[jax.random.permutation(jax.random.fold_in(own, 1), rows)]
    offset_by = jax.random.randint(jax.random.fold_in(own, 2), (rows, 1), 0, top)
    return jnp.take_along_axis(grid, (jnp.arange(top)[None, :] + offset_by) % top, axis=1)


def portions_of(amount, total, most, lean, full):
    weights = [(1 << 20) // math.isqrt(rank ** lean) + 1 for rank in range(1, amount + 1)]
    largest = most if full else min(most, max(-(-total // amount), total * weights[0] // sum(weights)))
    least = 1 if total - largest >= amount - 1 else 0
    holding, surplus = [largest] + [least] * (amount - 1), total - largest - least * (amount - 1)
    while surplus > 0:
        free = [i for i in range(1, amount) if holding[i] < largest] or [i for i in range(1, amount) if holding[i] < most]
        whole, remaining = sum([weights[i] for i in free]), surplus
        for i in free:
            more = min(most - holding[i], max(1, remaining * weights[i] // whole), surplus)
            holding[i] = holding[i] + more
            surplus = surplus - more
    return np.array(holding)


def scatter_about(key, shape, scale, bound, cuts=(), held_as=jnp.bfloat16):
    result = jax.random.normal(key, shape, jnp.float32) * scale
    if len(cuts) > 0:
        result = level_of(key, shape, cuts, -0.22, 0.18) * result
    return jnp.clip(result, min=-bound, max=bound).astype(held_as)


def setup_inputs(seed: int = 0) -> dict:
    keys = jax.random.split(jax.random.key(seed), 11)
    fine_atmospheric_values = scatter_about(keys[0], (FIELDS, FINE_EASTWARD, FINE_NORTHWARD), 1.0, 6.0, ((1, 4), (2, 8)), jnp.float32)
    fine_skin_heat = scatter_about(keys[1], (FINE_EASTWARD, FINE_NORTHWARD), 1.0, 6.0, ((0, 4), (1, 8)), jnp.float32)
    coarse_lowest_values = scatter_about(keys[2], (FIELDS, PARX, PARY), 1.0, 6.0, ((1, 4), (2, 8)))
    holder_flat = jax.random.randint(keys[3], (1,), 0, DEVICES).astype(jnp.int32)
    corner_offset = jax.random.randint(keys[4], (2,), 0, PC - max(WINX, WINY) + 1).astype(jnp.int32)
    exchange_patch_holder_keys = jax.random.split(jax.random.fold_in(keys[5], 1), TOTB // NB)
    exchange_patch_holder_turns = jax.random.permutation(jax.random.fold_in(keys[5], 3), TOTB // NB)
    exchange_patch_holder = jax.vmap(lambda own, number: routed_block(jax.random.fold_in(keys[5], 2), own, number, NB, DEVICES, 1, CAP, 2))(exchange_patch_holder_keys, exchange_patch_holder_turns).reshape((TOTB, 1))
    holder_patch_position = with_ends(jax.random.randint(keys[6], (TOTB,), 0, MARINE_PATCHES), jax.random.fold_in(keys[6], 1), 0, MARINE_PATCHES - 1).astype(jnp.int32)
    coarse_interface_exchange = scatter_about(keys[7], (FIELDS, OCEAN_CELLS), 1.0, 6.0, ((1, 32),), jnp.float32)
    marine_stratum_values = scatter_about(keys[8], (FIELDS, LAYERS, OCEAN_CELLS), 1.0, 6.0, ((2, 32),), jnp.float32)
    diffusion_solver_operator = draw_diffusion_solver_operator(jax.random.fold_in(keys[10], 71), 0)
    return {"fine_atmospheric_values": fine_atmospheric_values, "fine_skin_heat": fine_skin_heat, "coarse_lowest_values": coarse_lowest_values, "holder_flat": holder_flat, "corner_offset": corner_offset, "exchange_patch_holder": exchange_patch_holder, "holder_patch_position": holder_patch_position, "coarse_interface_exchange": coarse_interface_exchange, "marine_stratum_values": marine_stratum_values, "diffusion_solver_operator": diffusion_solver_operator}


diffuse_coef = 0.24
relax_coef = 0.3
drag_coefficient = 0.5

def hat_weights(cell_count, first_cell, anchor_cell, base_cell, parent_cells):
    fine_cells = (jnp.arange(cell_count) + first_cell).astype(jnp.float32)
    centre = (fine_cells + 0.5) * (2.0 / 13.0) - 0.5 + anchor_cell.astype(jnp.float32)
    coarse = (jnp.arange(parent_cells) + base_cell).astype(jnp.float32)
    return jnp.maximum(0.0, 1.0 - jnp.abs(centre[:, None] - coarse[None, :])).astype(jnp.bfloat16)

def reference(fine_atmospheric_values, fine_skin_heat, coarse_lowest_values, holder_flat, corner_offset, exchange_patch_holder, holder_patch_position, coarse_interface_exchange, marine_stratum_values, diffusion_solver_operator):
    row_owner = (holder_flat[0] // N_GY).astype(jnp.int32)
    col_owner = (holder_flat[0] % N_GY).astype(jnp.int32)
    zero_index = jnp.zeros((), jnp.int32)
    parent_block = lax.dynamic_slice(coarse_lowest_values, (zero_index, row_owner * PC, col_owner * PC), (FIELDS, PC, PC))
    weight_x = hat_weights(FINE_EASTWARD, 0, corner_offset[0], 0, PC)
    weight_y = hat_weights(FINE_NORTHWARD, 0, corner_offset[1], 0, PC)
    partial_value = jnp.einsum('fpq,jq->fpj', parent_block.astype(jnp.float32), weight_y.astype(jnp.float32)).astype(jnp.bfloat16)
    forcing = jnp.einsum('ip,fpj->fij', weight_x.astype(jnp.float32), partial_value.astype(jnp.float32))
    present_fine_values = fine_atmospheric_values
    for iteration in range(STEPS):
        padded = jnp.pad(present_fine_values, ((0, 0), (1, 1), (1, 1)))
        beside = padded[:, 2:, 1:-1] + padded[:, :-2, 1:-1] + padded[:, 1:-1, 2:] + padded[:, 1:-1, :-2]
        present_fine_values = present_fine_values + diffuse_coef * (beside - 4.0 * present_fine_values) + relax_coef * (forcing - present_fine_values)
    breeze_speed = jnp.sqrt(1.0 + present_fine_values[0] * present_fine_values[0] + present_fine_values[1] * present_fine_values[1])
    interface_exchange = jnp.stack([drag_coefficient * breeze_speed * (present_fine_values[2] - fine_skin_heat), drag_coefficient * breeze_speed * (present_fine_values[3] - 0.5 * fine_skin_heat), drag_coefficient * breeze_speed * present_fine_values[0], drag_coefficient * breeze_speed * present_fine_values[1]])
    tiles = interface_exchange.reshape(FIELDS, N_GX, CHIP_FINE_EAST, N_GY, CHIP_FINE_NORTH).transpose(1, 3, 0, 2, 4)
    blocks = tiles.reshape(N_GX * N_GY, FIELDS, NB, EXCHANGE_PATCH).transpose(0, 2, 1, 3).reshape(TOTB, FIELDS, EXCHANGE_PATCH)
    target_holder = exchange_patch_holder[:, 0] * MARINE_PATCHES + holder_patch_position
    group_tags = N_GX * N_GY * MARINE_PATCHES
    block_sums = jax.ops.segment_sum(blocks, target_holder, group_tags)
    counts = jax.ops.segment_sum(jnp.ones((TOTB,), jnp.float32), target_holder, group_tags)
    coarse = coarse_interface_exchange.reshape(FIELDS, group_tags, EXCHANGE_PATCH).transpose(1, 0, 2)
    uncovered = (counts == 0.0).astype(jnp.float32)
    forcing_ocean = (block_sums + coarse * uncovered[:, None, None]) / jnp.maximum(counts, 1.0)[:, None, None]
    forcing_cells = forcing_ocean.transpose(1, 0, 2).reshape(FIELDS, OCEAN_CELLS)
    forced = marine_stratum_values.at[:, 0, :].set(marine_stratum_values[:, 0, :] + forcing_cells)
    refreshed_marine_values = jnp.einsum('lk,fkc->flc', diffusion_solver_operator, forced, precision=lax.Precision.HIGHEST)
    skin_heat_gather = refreshed_marine_values[0, 0].reshape(group_tags, EXCHANGE_PATCH)
    returned_patches = skin_heat_gather[target_holder]
    fine_refreshed_skin_heat = returned_patches.reshape(N_GX, N_GY, CHIP_FINE_EAST, CHIP_FINE_NORTH).transpose(0, 2, 1, 3).reshape(FINE_EASTWARD, FINE_NORTHWARD)
    return (present_fine_values, refreshed_marine_values, fine_refreshed_skin_heat)
```

```python
import functools
import math

import jax
import jax.numpy as jnp
from jax import lax
from jax.experimental import pallas as pl
from jax.experimental.pallas import tpu as pltpu
from jax.sharding import PartitionSpec as P

FIELDS = 4
PATCH = 128
MARINE = 32
STEPS = 4
WROWS = 48
WCOLS = 32
HALO = 8
CHUNK = 256
DIFFUSE = 0.24
RELAX = 0.3
DRAG = 0.5
F32 = jnp.float32
BF16 = jnp.bfloat16
MESH = pl.DeviceIdType.MESH
NT = (((1,), (1,)), ((), ()))
TN = (((0,), (0,)), ((), ()))


def iota(shape, dim):
    return lax.broadcasted_iota(jnp.int32, shape, dim)


def hot(condition):
    return jnp.where(condition, 1.0, 0.0).astype(BF16)


def dot(a, b):
    return jnp.dot(a, b, preferred_element_type=F32)


def first_parent(first_fine):
    return (4 * first_fine - 11) // 26


def kernel(
    nx, ny, cap, jp, rp, yw,
    holder, corner, index_row, owner_col, fine, skin, coarse, exchange, marine, op,
    nest_out, marine_out, heat_out,
    centre, strips, rows_in, cols_in, corners_in,
    tx1, rx1, pmat, flux_tile, flux_rows, flux_pack, tx2, rx2, amat, qmat, tx3, rx3,
    marine_in, mixed, skin_base, coarse_rows,
    marine_sem, out_sem, local_sem, halo_send, halo_recv, send_sem, recv_sem,
):
    tile_x, tile_y = fine.shape[1], fine.shape[2]
    blocks = owner_col.shape[0]
    devices = nx * ny
    ix, iy = lax.axis_index("gx"), lax.axis_index("gy")
    me = ix * ny + iy

    barrier = pltpu.get_barrier_semaphore()

    def greet(t, carry):
        other = lax.rem(me + t, devices)
        pl.semaphore_signal(
            barrier, inc=1, device_id=(lax.div(other, ny), lax.rem(other, ny)), device_id_type=MESH
        )
        return carry

    lax.fori_loop(1, devices, greet, 0)
    marine_copy = pltpu.make_async_copy(marine, marine_in, marine_sem)
    marine_copy.start()

    for f in range(FIELDS):
        centre[f, :, :] = jnp.zeros((tile_x, PATCH), F32)
        centre[f, :, 0:tile_y] = fine[f]
    wide = jnp.concatenate([centre[f].astype(BF16) for f in range(FIELDS)], axis=1)
    r = iota((32, FIELDS * PATCH), 0)
    field_col = ((r & 15) >> 2) * PATCH + (r & 3)
    lane = iota((32, FIELDS * PATCH), 1)
    pick = hot(lane == field_col + jnp.where(r >= 16, tile_y - 4, 0))
    place = hot(lane == field_col + jnp.where(r >= 16, tile_y, PATCH - 4))
    wide = jnp.concatenate([wide, jnp.zeros((256 - tile_x, FIELDS * PATCH), BF16)], axis=0)
    strips[...] = lax.dot_general(pick, wide, NT, preferred_element_type=F32).astype(BF16)

    owner_row, pos_row = index_row[0:1, :], index_row[1:2, :]
    same = owner_col[...] == owner_row
    k0, k1 = iota((blocks, 256), 0), iota((blocks, 256), 1)
    rank_row = jnp.sum(jnp.where(same & (k0 < k1), 1.0, 0.0), axis=0, keepdims=True).astype(jnp.int32)
    rank_col = jnp.sum(jnp.where(same & (k1 < k0), 1.0, 0.0), axis=1, keepdims=True).astype(jnp.int32)

    owners_hot = jnp.where(iota((devices, 256), 0) == owner_row, 1.0, 0.0)
    weighted = (owners_hot * (pos_row + 1).astype(F32)).astype(BF16)
    j = iota((PATCH, 256), 0)
    field = sum([jnp.where(j >= n * cap, 1, 0) for n in range(1, FIELDS)])
    ranks_hot = hot((j - field * cap == rank_row) & (j < FIELDS * cap))
    slots = lax.dot_general(weighted, ranks_hot, NT, preferred_element_type=F32)
    j = iota((devices, PATCH), 1)
    field = sum([jnp.where(j >= n * cap, 1.0, 0.0) for n in range(1, FIELDS)])
    codes = jnp.where(slots > 0.5, slots + MARINE * field, 0.0)

    cells = coarse.shape[1]
    away = (holder[0] - me) * 65536
    q = iota((cells, yw), 0)
    choose_y = hot(q == iota((cells, yw), 1) + (corner[1] - 1))
    p = iota((WROWS, cells), 1) - iota((WROWS, cells), 0) - (corner[0] + away)
    choose_x = jnp.concatenate([hot(p == first_parent(a * tile_x - 3)) for a in range(nx)], axis=0)
    windows = []
    for f in range(FIELDS):
        narrow = dot(coarse[f], choose_y).astype(BF16)
        windows.append(dot(choose_x, narrow))
    lane_group = iota((nx * WROWS, PATCH), 1) // WCOLS
    piece_row = iota((WROWS, PATCH), 0)
    for b in range(ny):
        base = first_parent(b * tile_y - 3) + 1
        piece = jnp.zeros((nx * WROWS, PATCH), F32)
        for f in range(FIELDS):
            moved = pltpu.roll(windows[f], (f * WCOLS - base) % yw, 1)[:, 0:PATCH]
            piece = jnp.where(lane_group == f, moved, piece)
        for a in range(nx):
            d = a * ny + b
            part = piece[a * WROWS : (a + 1) * WROWS]
            tx1[d] = jnp.where(piece_row == WROWS - 1, codes[d : d + 1, :], part).astype(BF16)

    pl.semaphore_wait(barrier, devices - 1)

    def send(phase, source, target):
        def one(t, carry):
            other = lax.rem(me + t, devices)
            pltpu.make_async_remote_copy(
                src_ref=source(other),
                dst_ref=target,
                send_sem=send_sem.at[phase],
                recv_sem=recv_sem.at[phase],
                device_id=(lax.div(other, ny), lax.rem(other, ny)),
                device_id_type=MESH,
            ).start()
            return carry

        lax.fori_loop(1, devices, one, 0)

    def all_of(ref, rows, sem):
        whole = ref.at[pl.ds(0, (devices - 1) * rows)]
        pltpu.make_async_copy(whole, whole, sem).wait()

    west, east = lax.rem(ix + nx - 1, nx), lax.rem(ix + 1, nx)
    south, north = lax.rem(iy + ny - 1, ny), lax.rem(iy + 1, ny)
    left, right = pl.ds(0, 16), pl.ds(16, 16)
    low, high = pl.ds(0, 128), pl.ds(128, 128)
    halos = [
        (centre.at[:, pl.ds(tile_x - HALO, HALO), :], rows_in.at[0], (east, iy)),
        (centre.at[:, pl.ds(0, HALO), :], rows_in.at[1], (west, iy)),
        (strips.at[right], cols_in.at[left], (ix, north)),
        (strips.at[left], cols_in.at[right], (ix, south)),
        (strips.at[right, high], corners_in.at[0, left], (east, north)),
        (strips.at[left, high], corners_in.at[0, right], (east, south)),
        (strips.at[right, low], corners_in.at[1, left], (west, north)),
        (strips.at[left, low], corners_in.at[1, right], (west, south)),
    ]
    halos = [
        pltpu.make_async_remote_copy(
            src_ref=src, dst_ref=dst, send_sem=halo_send.at[n], recv_sem=halo_recv.at[n],
            device_id=where, device_id_type=MESH,
        )
        for n, (src, dst, where) in enumerate(halos)
    ]
    for copy in halos:
        copy.start()
    send(0, lambda other: tx1.at[other], rx1.at[me])
    own1 = pltpu.make_async_copy(tx1.at[me], rx1.at[me], local_sem)
    own1.start()

    target = owner_row * jp + rank_row

    def dispatch_rows(c, carry):
        start = pl.multiple_of(c * CHUNK, CHUNK)
        row = iota((CHUNK, 256), 0) + start
        for f in range(FIELDS):
            pmat[pl.ds(start, CHUNK), f * 256 : (f + 1) * 256] = hot(row == target + f * cap)
        return carry

    lax.fori_loop(0, devices * jp // CHUNK, dispatch_rows, 0)
    flux_pack[...] = jnp.zeros(flux_pack.shape, BF16)

    op_high = op[...].astype(BF16)
    op_low = (op[...] - op_high.astype(F32)).astype(BF16)
    marine_copy.wait()
    width = 512
    for f in range(FIELDS):

        def mix(c, carry, f=f):
            columns = pl.ds(pl.multiple_of(c * width, width), width)
            value = marine_in[f, :, columns]
            m_high = value.astype(BF16)
            m_low = (value - m_high.astype(F32)).astype(BF16)
            mixed[f, :, columns] = dot(op_high, m_high) + (dot(op_low, m_high) + dot(op_high, m_low))
            return carry

        lax.fori_loop(0, marine_in.shape[2] // width, mix, 0)
    for g in range(MARINE):
        skin_base[g : g + 1, :] = mixed[0, 0:1, g * PATCH : (g + 1) * PATCH]
        for f in range(FIELDS):
            coarse_rows[f * MARINE + g : f * MARINE + g + 1, :] = exchange[f : f + 1, g * PATCH : (g + 1) * PATCH]

    own1.wait()
    all_of(rx1, 1, recv_sem.at[0])
    for copy in halos:
        copy.wait()
    all_of(tx1, 1, send_sem.at[0])

    window = lax.fori_loop(
        0, devices, lambda s, total: total + rx1[s].astype(F32), jnp.zeros((WROWS, PATCH), F32)
    ).astype(BF16)
    height = tile_x + 2 * HALO
    fx = (iota((height, WROWS), 0) + (ix * tile_x - HALO)).astype(F32)
    first_x = (4 * (ix * tile_x - 3) - 11 + 26) // 26 - 1
    at_x = (fx + 0.5) * (2.0 / 13.0) - 0.5 + corner[0].astype(F32)
    px = (iota((height, WROWS), 1) + (first_x + corner[0])).astype(F32)
    wx = jnp.maximum(0.0, 1.0 - jnp.abs(at_x - px)).astype(BF16)
    lane_y = iota((PATCH, PATCH), 0)
    lane_y = lane_y - jnp.where(lane_y >= PATCH - 16, PATCH, 0)
    fy = (lane_y + iy * tile_y).astype(F32)
    first_y = (4 * (iy * tile_y - 3) - 11 + 26) // 26 - 1
    at_y = (fy + 0.5) * (2.0 / 13.0) - 0.5 + corner[1].astype(F32)
    py = ((iota((PATCH, PATCH), 1) & (WCOLS - 1)) + (first_y + corner[1])).astype(F32)
    wy = jnp.maximum(0.0, 1.0 - jnp.abs(at_y - py))
    group_y = iota((PATCH, PATCH), 1) // WCOLS

    side = lax.dot_general(cols_in[...], place, TN, preferred_element_type=F32)
    side_low = lax.dot_general(corners_in[0], place, TN, preferred_element_type=F32)
    side_high = lax.dot_general(corners_in[1], place, TN, preferred_element_type=F32)

    gi = iota((height, PATCH), 0) + (ix * tile_x - HALO)
    gj = iota((height, PATCH), 1)
    gj = gj - jnp.where(gj >= PATCH - 16, PATCH, 0) + iy * tile_y
    inside = (gi >= 0) & (gi < nx * tile_x) & (gj >= 0) & (gj < ny * tile_y)
    final = []
    for f in range(FIELDS):
        wy_f = jnp.where(group_y == f, wy, 0.0).astype(BF16)
        partial = lax.dot_general(window, wy_f, NT, preferred_element_type=F32).astype(BF16)
        forcing = dot(wx, partial)
        cut = slice(f * PATCH, (f + 1) * PATCH)
        state = jnp.concatenate(
            [
                rows_in[0, f] + side_low[56:64, cut],
                centre[f] + side[0:tile_x, cut],
                rows_in[1, f] + side_high[0:8, cut],
            ],
            axis=0,
        )
        state = jnp.where(inside, state, 0.0)
        for _ in range(STEPS):
            beside = (
                pltpu.roll(state, 1, 0) + pltpu.roll(state, height - 1, 0)
                + pltpu.roll(state, 1, 1) + pltpu.roll(state, PATCH - 1, 1)
            )
            state = state + DIFFUSE * (beside - 4.0 * state) + RELAX * (forcing - state)
            state = jnp.where(inside, state, 0.0)
        state = state[HALO : HALO + tile_x]
        nest_out[f] = state[:, 0:tile_y]
        final.append(state)

    flux_tile[:, 0:tile_y] = skin[...]
    heat = flux_tile[...]
    u, v, ta, qa = final
    drag = DRAG * jnp.sqrt(1.0 + u * u + v * v)
    lane = iota((tile_x // 4, PATCH), 1)
    for f, flux in enumerate((drag * (ta - heat), drag * (qa - 0.5 * heat), drag * u, drag * v)):
        flux_tile[...] = flux
        f0, f1, f2, f3 = [flux_tile[pl.ds(n, tile_x // 4, stride=4), :] for n in range(4)]
        f1, f2 = pltpu.roll(f1, 96, 1), pltpu.roll(f2, 64, 1)
        flux_rows[pl.ds(0, blocks // 3, stride=3), :] = jnp.where(lane < 96, f0, f1)
        flux_rows[pl.ds(1, blocks // 3, stride=3), :] = jnp.where(lane < 64, f1, f2)
        flux_rows[pl.ds(2, blocks // 3, stride=3), :] = jnp.where(lane < 32, f2, pltpu.roll(f3, 32, 1))
        flux_pack[f * 256 : f * 256 + blocks, :] = flux_rows[...].astype(BF16)

    def dispatch(c, carry):
        rows = pl.ds(pl.multiple_of(c * CHUNK, CHUNK), CHUNK)
        tx2[rows, :] = dot(pmat[rows, :], flux_pack[...]).astype(BF16)
        return carry

    lax.fori_loop(0, devices * jp // CHUNK, dispatch, 0)

    def part(ref, device, rows):
        return ref.at[pl.ds(pl.multiple_of(device * rows, 16), rows)]

    send(1, lambda other: part(tx2, other, jp), part(rx2, me, jp))
    own2 = pltpu.make_async_copy(part(tx2, me, jp), part(rx2, me, jp), local_sem)
    own2.start()

    got = rx1[:, WROWS - 16 : WROWS, :].astype(F32)[:, 15, :].astype(BF16)

    def spread_codes(pitch, limit):
        period = math.lcm(pitch, PATCH)
        a, b = iota((PATCH, period), 0), iota((PATCH, period), 1)
        repeat = functools.reduce(
            jnp.logical_or, [b == a + n * pitch for n in range(period // pitch)]
        ) & (a < limit)
        tiled = dot(got, hot(repeat))
        tiled = jnp.concatenate([tiled] * (devices * pitch // period), axis=1)
        s, l = iota(tiled.shape, 0), iota(tiled.shape, 1)
        mine = (l >= s * pitch) & (l < (s + 1) * pitch)
        return jnp.sum(jnp.where(mine, tiled, 0.0), axis=0, keepdims=True).astype(jnp.int32) - 1

    code = spread_codes(jp, FIELDS * cap)
    amat[...] = hot(iota((FIELDS * MARINE, devices * jp), 0) == code)
    count = jnp.sum(amat[0:MARINE, :].astype(F32), axis=1, keepdims=True)
    code = spread_codes(rp, cap)
    qmat[...] = hot(iota((MARINE, devices * rp), 0) == code)

    own2.wait()
    all_of(rx2, jp, recv_sem.at[1])
    all_of(tx2, jp, send_sem.at[1])
    sums = dot(amat[...], rx2[...])
    least = jnp.maximum(count, 1.0)
    empty = jnp.where(count == 0.0, 1.0, 0.0)
    forced = [
        (sums[f * MARINE : (f + 1) * MARINE] + coarse_rows[f * MARINE : (f + 1) * MARINE, :] * empty) / least
        for f in range(FIELDS)
    ]
    new_skin = (skin_base[...] + op[0:1, 0:1] * forced[0]).astype(BF16)
    tx3[...] = lax.dot_general(qmat[...], new_skin, TN, preferred_element_type=F32).astype(BF16)
    send(2, lambda other: part(tx3, other, rp), part(rx3, me, rp))
    own3 = pltpu.make_async_copy(part(tx3, me, rp), part(rx3, me, rp), local_sem)
    own3.start()

    first = op[:, 0:1]
    for f in range(FIELDS):
        for g in range(MARINE):
            cut = slice(g * PATCH, (g + 1) * PATCH)
            mixed[f, :, cut] = mixed[f, :, cut] + first * forced[f][g : g + 1, :]
    marine_back = pltpu.make_async_copy(mixed, marine_out, out_sem)
    marine_back.start()
    where_from = hot(iota((blocks, devices * rp), 1) == owner_col[...] * rp + rank_col)
    own3.wait()
    all_of(rx3, rp, recv_sem.at[2])
    all_of(tx3, rp, send_sem.at[2])
    heat_out[...] = dot(where_from, rx3[...])
    marine_back.wait()


def on_device(nx, ny, fine, skin, coarse, holder, corner, owner, position, exchange, marine, op):
    devices = nx * ny
    tile_x, tile_y = fine.shape[1:]
    blocks = tile_x * tile_y // PATCH
    cap = max(2, (2 * blocks + devices - 1) // devices)
    jp = -(-FIELDS * cap // 16) * 16
    rp = -(-cap // 16) * 16
    last = first_parent((ny - 1) * tile_y - 3) + 1 + 18
    yw = -(-last // PATCH) * PATCH
    layers, cells = marine.shape[1:]
    index_row = jnp.pad(
        jnp.stack([owner[:, 0], position]), ((0, 0), (0, 256 - blocks)), constant_values=-1
    )
    vmem = pl.BlockSpec(memory_space=pltpu.VMEM)
    smem = pl.BlockSpec(memory_space=pltpu.SMEM)
    anywhere = pl.BlockSpec(memory_space=pl.ANY)
    nest, marine_new, heat = pl.pallas_call(
        functools.partial(kernel, nx, ny, cap, jp, rp, yw),
        out_shape=(
            jax.ShapeDtypeStruct(fine.shape, F32),
            jax.ShapeDtypeStruct(marine.shape, F32),
            jax.ShapeDtypeStruct((blocks, PATCH), F32),
        ),
        in_specs=[smem, smem, vmem, vmem, vmem, vmem, vmem, vmem, anywhere, vmem],
        out_specs=(vmem, anywhere, vmem),
        scratch_shapes=[
            pltpu.VMEM((FIELDS, tile_x, PATCH), F32),
            pltpu.VMEM((32, 256), BF16),
            pltpu.VMEM((2, FIELDS, HALO, PATCH), F32),
            pltpu.VMEM((32, 256), BF16),
            pltpu.VMEM((2, 32, PATCH), BF16),
            pltpu.VMEM((devices, WROWS, PATCH), BF16),
            pltpu.VMEM((devices, WROWS, PATCH), BF16),
            pltpu.VMEM((devices * jp, FIELDS * 256), BF16),
            pltpu.VMEM((tile_x, PATCH), F32),
            pltpu.VMEM((blocks, PATCH), F32),
            pltpu.VMEM((FIELDS * 256, PATCH), BF16),
            pltpu.VMEM((devices * jp, PATCH), BF16),
            pltpu.VMEM((devices * jp, PATCH), BF16),
            pltpu.VMEM((FIELDS * MARINE, devices * jp), BF16),
            pltpu.VMEM((MARINE, devices * rp), BF16),
            pltpu.VMEM((devices * rp, PATCH), BF16),
            pltpu.VMEM((devices * rp, PATCH), BF16),
            pltpu.VMEM((FIELDS, layers, cells), F32),
            pltpu.VMEM((FIELDS, layers, cells), F32),
            pltpu.VMEM((MARINE, PATCH), F32),
            pltpu.VMEM((FIELDS * MARINE, PATCH), F32),
            pltpu.SemaphoreType.DMA,
            pltpu.SemaphoreType.DMA,
            pltpu.SemaphoreType.DMA,
            pltpu.SemaphoreType.DMA((8,)),
            pltpu.SemaphoreType.DMA((8,)),
            pltpu.SemaphoreType.DMA((3,)),
            pltpu.SemaphoreType.DMA((3,)),
        ],
        compiler_params=pltpu.CompilerParams(
            collective_id=0, has_side_effects=True, vmem_limit_bytes=40 * 1024 * 1024
        ),
    )(holder, corner, index_row, owner, fine, skin, coarse, exchange, marine, op)
    return nest, marine_new, heat.reshape(tile_x, tile_y)


def solution(mesh):
    in_specs = (
        P(None, "gx", "gy"),
        P("gx", "gy"),
        P(None, "gx", "gy"),
        P(),
        P(),
        P(("gx", "gy"), None),
        P(("gx", "gy")),
        P(None, ("gx", "gy")),
        P(None, None, ("gx", "gy")),
        P(),
    )
    out_specs = (P(None, "gx", "gy"), P(None, None, ("gx", "gy")), P("gx", "gy"))
    return jax.shard_map(
        functools.partial(on_device, mesh.shape["gx"], mesh.shape["gy"]),
        mesh=mesh,
        in_specs=in_specs,
        out_specs=out_specs,
        check_vma=False,
    )
```

```python
import functools
import math

import jax
import jax.numpy as jnp
from jax import lax
from jax.experimental import pallas as pl
from jax.experimental.pallas import tpu as pltpu
from jax.sharding import PartitionSpec as P

FIELDS = 4
PATCH = 128
MARINE = 32
STEPS = 4
WCOLS = 32
SLOT_LANE = 18
HALO = 8
DIFFUSE = 0.24
RELAX = 0.3
DRAG = 0.5
F32 = jnp.float32
BF16 = jnp.bfloat16
MESH = pl.DeviceIdType.MESH
NT = (((1,), (1,)), ((), ()))
TN = (((0,), (0,)), ((), ()))


def iota(shape, dim):
    return lax.broadcasted_iota(jnp.int32, shape, dim)


def hot(condition):
    return jnp.where(condition, 1.0, 0.0).astype(BF16)


def dot(a, b):
    return jnp.dot(a, b, preferred_element_type=F32)


def first_parent(first_fine):
    return (4 * first_fine - 11) // 26


def kernel(
    nx, ny, cap, jp, rp, yw, wrows, per,
    holder, corner, owner, position, fine, skin, coarse_far, exchange, marine, op,
    nest_out, marine_out, heat_out,
    coarse, index_row, centre, strips, rows_in, cols_in, corners_in,
    tx1, rx1, pmat, flux_tile, flux_rows, flux_pack, tx2, rx2, amat, qmat, tx3, rx3,
    marine_in, mixed, op_column, coarse_rows, forced,
    marine_sem, out_sem, local_sem, halo_send, halo_recv, send_sem, recv_sem,
):
    tile_x, tile_y = fine.shape[1], fine.shape[2]
    blocks = owner.shape[1]
    layers = op.shape[0]
    devices = nx * ny
    ix, iy = lax.axis_index("gx"), lax.axis_index("gy")
    me = ix * ny + iy

    coarse_copy = pltpu.make_async_copy(coarse_far, coarse, local_sem.at[0])
    coarse_copy.start()
    rx3[...] = jnp.zeros(rx3.shape, F32)
    barrier = pltpu.get_barrier_semaphore()

    def greet(t, carry):
        other = lax.rem(me + t, devices)
        pl.semaphore_signal(
            barrier, inc=1, device_id=(lax.div(other, ny), lax.rem(other, ny)), device_id_type=MESH
        )
        return carry

    lax.fori_loop(1, devices, greet, 0)

    def ocean_block(ref, g):
        return ref.at[:, :, pl.ds(pl.multiple_of(g * PATCH, PATCH), PATCH)]

    def fetch(g):
        return pltpu.make_async_copy(
            ocean_block(marine, g), marine_in.at[g, :, pl.ds(0, FIELDS), :], marine_sem.at[g]
        )

    def keep(g):
        return pltpu.make_async_copy(
            mixed.at[g, :, pl.ds(0, FIELDS), :], ocean_block(marine_out, g), out_sem.at[g]
        )

    def each(count, work):
        def one(n, carry):
            work(n)
            return carry

        lax.fori_loop(0, count, one, 0)

    each(MARINE, lambda g: fetch(g).start())

    for f in range(FIELDS):
        centre[f, :, :] = jnp.zeros((tile_x, PATCH), F32)
        centre[f, :, 0:tile_y] = fine[f]
    wide = jnp.concatenate([centre[f].astype(BF16) for f in range(FIELDS)], axis=1)
    r = iota((32, FIELDS * PATCH), 0)
    field_col = ((r & 15) >> 2) * PATCH + (r & 3)
    lane = iota((32, FIELDS * PATCH), 1)
    pick = hot(lane == field_col + jnp.where(r >= 16, tile_y - 4, 0))
    place = hot(lane == field_col + jnp.where(r >= 16, tile_y, PATCH - 4))
    wide = jnp.concatenate([wide, jnp.zeros((256 - tile_x, FIELDS * PATCH), BF16)], axis=0)
    strips[...] = lax.dot_general(pick, wide, NT, preferred_element_type=F32).astype(BF16)

    index_row[...] = jnp.full(index_row.shape, -1, jnp.int32)
    index_row[0:1, 0:blocks] = owner[...]
    index_row[1:2, 0:blocks] = position[...]
    owner_row, pos_row = index_row[0:1, :], index_row[1:2, :]
    k0, k1 = iota((blocks, 256), 0), iota((blocks, 256), 1)
    owner_col = jnp.sum(
        jnp.where(k0 == k1, owner_row.astype(F32), 0.0), axis=1, keepdims=True
    ).astype(jnp.int32)
    same = owner_col == owner_row
    rank_row = jnp.sum(jnp.where(same & (k0 < k1), 1.0, 0.0), axis=0, keepdims=True).astype(jnp.int32)
    rank_col = jnp.sum(jnp.where(same & (k1 < k0), 1.0, 0.0), axis=1, keepdims=True).astype(jnp.int32)

    owners_hot = jnp.where(iota((devices, 256), 0) == owner_row, 1.0, 0.0)
    weighted = (owners_hot * (pos_row + 1).astype(F32)).astype(BF16)
    ranks_hot = hot(iota((PATCH, 256), 0) - SLOT_LANE == rank_row)
    slots = lax.dot_general(weighted, ranks_hot, NT, preferred_element_type=F32)

    coarse_copy.wait()
    cells = coarse.shape[1]
    away = (holder[0] - me) * 65536
    q = iota((cells, yw), 0)
    choose_y = hot(q == iota((cells, yw), 1) + (corner[1] - 1))
    p = iota((wrows, cells), 1) - iota((wrows, cells), 0) - (corner[0] + away)
    choose_x = jnp.concatenate([hot(p == first_parent(a * tile_x - 3)) for a in range(nx)], axis=0)
    windows = []
    for f in range(FIELDS):
        narrow = dot(coarse[f], choose_y).astype(BF16)
        windows.append(dot(choose_x, narrow))
    lane_group = iota((nx * wrows, PATCH), 1) // WCOLS
    lane = iota((wrows, PATCH), 1)
    slot_place = (iota((wrows, PATCH), 0) == 0) & (lane >= SLOT_LANE) & (lane < WCOLS)
    for b in range(ny):
        base = first_parent(b * tile_y - 3) + 1
        piece = jnp.zeros((nx * wrows, PATCH), F32)
        for f in range(FIELDS):
            moved = pltpu.roll(windows[f], (f * WCOLS - base) % yw, 1)[:, 0:PATCH]
            piece = jnp.where(lane_group == f, moved, piece)
        for a in range(nx):
            d = a * ny + b
            part = piece[a * wrows : (a + 1) * wrows]
            tx1[d] = jnp.where(slot_place, slots[d : d + 1, :], part).astype(BF16)

    pl.semaphore_wait(barrier, devices - 1)

    def send(phase, source, target):
        def one(t, carry):
            other = lax.rem(me + t, devices)
            pltpu.make_async_remote_copy(
                src_ref=source(other),
                dst_ref=target,
                send_sem=send_sem.at[phase],
                recv_sem=recv_sem.at[phase],
                device_id=(lax.div(other, ny), lax.rem(other, ny)),
                device_id_type=MESH,
            ).start()
            return carry

        lax.fori_loop(1, devices, one, 0)

    def all_of(ref, sem):
        pltpu.make_async_copy(ref, ref, sem).wait()

    def others(ref, rows):
        return ref.at[pl.ds(0, (devices - 1) * rows)]

    west, east = lax.rem(ix + nx - 1, nx), lax.rem(ix + 1, nx)
    south, north = lax.rem(iy + ny - 1, ny), lax.rem(iy + 1, ny)
    left, right = pl.ds(0, 16), pl.ds(16, 16)
    low, high = pl.ds(0, 128), pl.ds(128, 128)
    halos = [
        (centre.at[:, pl.ds(tile_x - HALO, HALO), :], rows_in.at[0], (east, iy)),
        (centre.at[:, pl.ds(0, HALO), :], rows_in.at[1], (west, iy)),
        (strips.at[right], cols_in.at[left], (ix, north)),
        (strips.at[left], cols_in.at[right], (ix, south)),
        (strips.at[right, high], corners_in.at[0, left], (east, north)),
        (strips.at[left, high], corners_in.at[0, right], (east, south)),
        (strips.at[right, low], corners_in.at[1, left], (west, north)),
        (strips.at[left, low], corners_in.at[1, right], (west, south)),
    ]
    halos = [
        pltpu.make_async_remote_copy(
            src_ref=src, dst_ref=dst, send_sem=halo_send.at[n], recv_sem=halo_recv.at[n],
            device_id=where, device_id_type=MESH,
        )
        for n, (src, dst, where) in enumerate(halos)
    ]
    for copy in halos:
        copy.start()
    send(0, lambda other: tx1.at[other], rx1.at[me])
    own1 = pltpu.make_async_copy(tx1.at[me], rx1.at[me], local_sem.at[1])
    own1.start()

    target = owner_row * jp + rank_row

    chunk = per * jp

    def dispatch_rows(c):
        start = pl.multiple_of(c * chunk, chunk)
        row = iota((chunk, 256), 0) + start
        for f in range(FIELDS):
            pmat[pl.ds(start, chunk), f * 256 : (f + 1) * 256] = hot(row == target + f * cap)

    each(devices // per, dispatch_rows)
    flux_pack[...] = jnp.zeros(flux_pack.shape, BF16)

    op_high = op[...].astype(BF16)
    op_low = (op[...] - op_high.astype(F32)).astype(BF16)
    pitch = layers * 8
    marine_rows = marine_in.reshape(MARINE * pitch, PATCH)
    mixed_rows = mixed.reshape(MARINE * pitch, PATCH)

    def mix(c):
        for n in range(4):
            fetch(4 * c + n).wait()
        for f in range(FIELDS):
            rows = [pl.ds((4 * c + n) * pitch + f, layers, stride=8) for n in range(4)]
            value = jnp.concatenate([marine_rows[at, :] for at in rows], axis=1)
            m_high = value.astype(BF16)
            m_low = (value - m_high.astype(F32)).astype(BF16)
            value = dot(op_high, m_high) + (dot(op_low, m_high) + dot(op_high, m_low))
            for n, at in enumerate(rows):
                mixed_rows[at, :] = value[:, n * PATCH : (n + 1) * PATCH]

    each(MARINE // 4, mix)
    column = jnp.broadcast_to(op[:, 0:1], (layers, PATCH))
    for f in range(8):
        op_column[pl.ds(f, layers, stride=8), :] = column
    coarse_rows[...] = jnp.zeros(coarse_rows.shape, F32)
    for g in range(MARINE):
        coarse_rows[g * 8 : g * 8 + FIELDS, :] = exchange[:, g * PATCH : (g + 1) * PATCH]

    own1.wait()
    all_of(others(rx1, 1), recv_sem.at[0])
    for copy in halos:
        copy.wait_recv()

    window = lax.fori_loop(
        0, devices, lambda s, total: total + rx1[s].astype(F32), jnp.zeros((wrows, PATCH), F32)
    ).astype(BF16)
    height = tile_x + 2 * HALO
    fx = (iota((height, wrows), 0) + (ix * tile_x - HALO)).astype(F32)
    first_x = (4 * (ix * tile_x - 3) - 11 + 26) // 26 - 1
    at_x = (fx + 0.5) * (2.0 / 13.0) - 0.5 + corner[0].astype(F32)
    px = (iota((height, wrows), 1) + (first_x + corner[0])).astype(F32)
    wx = jnp.maximum(0.0, 1.0 - jnp.abs(at_x - px)).astype(BF16)
    lane_y = iota((PATCH, PATCH), 0)
    lane_y = lane_y - jnp.where(lane_y >= PATCH - 16, PATCH, 0)
    fy = (lane_y + iy * tile_y).astype(F32)
    first_y = (4 * (iy * tile_y - 3) - 11 + 26) // 26 - 1
    at_y = (fy + 0.5) * (2.0 / 13.0) - 0.5 + corner[1].astype(F32)
    py = ((iota((PATCH, PATCH), 1) & (WCOLS - 1)) + (first_y + corner[1])).astype(F32)
    wy = jnp.maximum(0.0, 1.0 - jnp.abs(at_y - py))
    group_y = iota((PATCH, PATCH), 1) // WCOLS

    side = lax.dot_general(cols_in[...], place, TN, preferred_element_type=F32)
    side_low = lax.dot_general(corners_in[0], place, TN, preferred_element_type=F32)
    side_high = lax.dot_general(corners_in[1], place, TN, preferred_element_type=F32)

    gi = iota((height, PATCH), 0) + (ix * tile_x - HALO)
    gj = iota((height, PATCH), 1)
    gj = gj - jnp.where(gj >= PATCH - 16, PATCH, 0) + iy * tile_y
    inside = (gi >= 0) & (gi < nx * tile_x) & (gj >= 0) & (gj < ny * tile_y)
    final = []
    for f in range(FIELDS):
        wy_f = jnp.where(group_y == f, wy, 0.0).astype(BF16)
        partial = lax.dot_general(window, wy_f, NT, preferred_element_type=F32).astype(BF16)
        forcing = dot(wx, partial)
        cut = slice(f * PATCH, (f + 1) * PATCH)
        state = jnp.concatenate(
            [
                rows_in[0, f] + side_low[56:64, cut],
                centre[f] + side[0:tile_x, cut],
                rows_in[1, f] + side_high[0:8, cut],
            ],
            axis=0,
        )
        state = jnp.where(inside, state, 0.0)
        for _ in range(STEPS):
            beside = (
                pltpu.roll(state, 1, 0) + pltpu.roll(state, height - 1, 0)
                + pltpu.roll(state, 1, 1) + pltpu.roll(state, PATCH - 1, 1)
            )
            state = state + DIFFUSE * (beside - 4.0 * state) + RELAX * (forcing - state)
            state = jnp.where(inside, state, 0.0)
        state = state[HALO : HALO + tile_x]
        nest_out[f] = state[:, 0:tile_y]
        final.append(state)

    flux_tile[:, 0:tile_y] = skin[...]
    heat = flux_tile[...]
    u, v, ta, qa = final
    drag = DRAG * jnp.sqrt(1.0 + u * u + v * v)
    lane = iota((tile_x // 4, PATCH), 1)
    for f, flux in enumerate((drag * (ta - heat), drag * (qa - 0.5 * heat), drag * u, drag * v)):
        flux_tile[...] = flux
        f0, f1, f2, f3 = [flux_tile[pl.ds(n, tile_x // 4, stride=4), :] for n in range(4)]
        f1, f2 = pltpu.roll(f1, 96, 1), pltpu.roll(f2, 64, 1)
        flux_rows[pl.ds(0, blocks // 3, stride=3), :] = jnp.where(lane < 96, f0, f1)
        flux_rows[pl.ds(1, blocks // 3, stride=3), :] = jnp.where(lane < 64, f1, f2)
        flux_rows[pl.ds(2, blocks // 3, stride=3), :] = jnp.where(lane < 32, f2, pltpu.roll(f3, 32, 1))
        flux_pack[f * 256 : f * 256 + blocks, :] = flux_rows[...].astype(BF16)

    def part(ref, device, rows):
        return ref.at[pl.ds(pl.multiple_of(device * rows, 16), rows)]

    def flux_to(other):
        return pltpu.make_async_remote_copy(
            src_ref=part(tx2, other, jp),
            dst_ref=part(rx2, me, jp),
            send_sem=send_sem.at[1],
            recv_sem=recv_sem.at[1],
            device_id=(lax.div(other, ny), lax.rem(other, ny)),
            device_id_type=MESH,
        )

    def dispatch(c):
        turn = lax.rem(c + lax.div(me, per), devices // per)
        rows = pl.ds(pl.multiple_of(turn * chunk, chunk), chunk)
        tx2[rows, :] = dot(pmat[rows, :], flux_pack[...]).astype(BF16)
        for n in range(per):
            other = turn * per + n

            @pl.when(other != me)
            def _():
                flux_to(other).start()

    each(devices // per, dispatch)
    own2 = pltpu.make_async_copy(part(tx2, me, jp), part(rx2, me, jp), local_sem.at[2])
    own2.start()

    got = rx1[:, 0:16, :].astype(F32)[:, 0, :].astype(BF16)

    def spread_slots(pitch, fields):
        period = math.lcm(pitch, PATCH)
        a, b = iota((PATCH, period), 0) - SLOT_LANE, iota((PATCH, period), 1)
        rank = b - pitch * sum([jnp.where(b >= n * pitch, 1, 0) for n in range(1, period // pitch)])
        inner = sum([jnp.where(rank >= f * cap, 1, 0) for f in range(1, fields + 1)])
        tiled = dot(got, hot((a == rank - inner * cap) & (a >= 0) & (inner < fields)))
        tiled = jnp.where(tiled > 0.5, tiled * 8.0 + inner[0:1].astype(F32), 0.0)
        tiled = jnp.concatenate([tiled] * (devices * pitch // period), axis=1)
        s, l = iota(tiled.shape, 0), iota(tiled.shape, 1)
        mine = (l >= s * pitch) & (l < (s + 1) * pitch)
        return jnp.sum(jnp.where(mine, tiled, 0.0), axis=0, keepdims=True).astype(jnp.int32) - 8

    amat[...] = hot(iota((MARINE * 8, devices * jp), 0) == spread_slots(jp, FIELDS))
    count = jnp.sum(amat[...].astype(F32), axis=1, keepdims=True)
    qmat[...] = hot(iota((MARINE, devices * rp), 0) * 8 == spread_slots(rp, 1))
    least = jnp.maximum(count, 1.0)
    empty = jnp.where(count == 0.0, coarse_rows[...], 0.0)
    skin_base = mixed_rows[pl.ds(0, MARINE, stride=pitch), :]

    own2.wait()
    all_of(others(rx2, jp), recv_sem.at[1])
    forced[...] = (dot(amat[...], rx2[...]) + empty) / least
    new_skin = skin_base + op[0:1, 0:1] * forced[pl.ds(0, MARINE, stride=8), :]

    def select(matrix, value, dims):
        high = value.astype(BF16)
        low = (value - high.astype(F32)).astype(BF16)
        both = lax.dot_general(
            matrix, jnp.concatenate([high, low], axis=1), dims, preferred_element_type=F32
        )
        return both[:, 0:PATCH] + both[:, PATCH:]

    tx3[...] = select(qmat[...], new_skin, TN).reshape(tx3.shape)
    send(2, lambda other: tx3.at[other, pl.ds(0, cap)], rx3.at[me, pl.ds(0, cap)])
    own3 = pltpu.make_async_copy(tx3.at[me, pl.ds(0, cap)], rx3.at[me, pl.ds(0, cap)], local_sem.at[3])
    own3.start()

    column = op_column[...].reshape(layers, 8, PATCH)

    def force(g):
        mixed[g] = mixed[g] + column * forced[pl.ds(pl.multiple_of(g * 8, 8), 8), :][None]
        keep(g).start()

    each(MARINE, force)
    where_from = hot(iota((blocks, devices * rp), 1) == owner_col * rp + rank_col)
    for copy in halos:
        copy.wait_send()
    all_of(others(tx1, 1), send_sem.at[0])
    all_of(others(tx2, jp), send_sem.at[1])
    own3.wait()
    all_of(rx3.at[pl.ds(0, devices - 1), pl.ds(0, cap)], recv_sem.at[2])
    flux_rows[...] = select(where_from, rx3[...].reshape(devices * rp, PATCH), (((1,), (0,)), ((), ())))
    h0, h1, h2 = [flux_rows[pl.ds(n, blocks // 3, stride=3), :] for n in range(3)]
    h1 = pltpu.roll(h1, 64, 1)
    quarter = tile_x // 4
    flux_tile[pl.ds(0, quarter, stride=4), :] = h0
    flux_tile[pl.ds(1, quarter, stride=4), :] = jnp.where(
        lane < 32, pltpu.roll(h0, 32, 1), pltpu.roll(h1, 96, 1)
    )
    flux_tile[pl.ds(2, quarter, stride=4), :] = jnp.where(lane < 64, h1, pltpu.roll(h2, 64, 1))
    flux_tile[pl.ds(3, quarter, stride=4), :] = pltpu.roll(h2, 96, 1)
    heat_out[...] = flux_tile[:, 0:tile_y]
    all_of(tx3.at[pl.ds(0, devices - 1), pl.ds(0, cap)], send_sem.at[2])
    each(MARINE, lambda g: keep(g).wait())


def on_device(nx, ny, fine, skin, coarse, holder, corner, owner, position, exchange, marine, op):
    devices = nx * ny
    tile_x, tile_y = fine.shape[1:]
    blocks = tile_x * tile_y // PATCH
    cap = max(2, (2 * blocks + devices - 1) // devices)
    jp = -(-FIELDS * cap // 16) * 16
    rp = -(-cap // 16) * 16
    spans = [
        first_parent(min((a + 1) * tile_x + 2, nx * tile_x - 1)) - first_parent(a * tile_x - 3) + 2
        for a in range(nx)
    ]
    wrows = -(-max(spans) // 16) * 16
    per = 2 ** int(math.log2(256 // jp))
    last = first_parent((ny - 1) * tile_y - 3) + 1 + 18
    yw = -(-last // PATCH) * PATCH
    layers, cells = marine.shape[1:]
    vmem = pl.BlockSpec(memory_space=pltpu.VMEM)
    smem = pl.BlockSpec(memory_space=pltpu.SMEM)
    anywhere = pl.BlockSpec(memory_space=pl.ANY)
    nest, marine_new, heat = pl.pallas_call(
        functools.partial(kernel, nx, ny, cap, jp, rp, yw, wrows, per),
        out_shape=(
            jax.ShapeDtypeStruct(fine.shape, F32),
            jax.ShapeDtypeStruct((layers, FIELDS, cells), F32),
            jax.ShapeDtypeStruct(skin.shape, F32),
        ),
        in_specs=[smem, smem, vmem, vmem, vmem, vmem, anywhere, vmem, anywhere, vmem],
        out_specs=(vmem, anywhere, vmem),
        scratch_shapes=[
            pltpu.VMEM(coarse.shape, BF16),
            pltpu.VMEM((8, 256), jnp.int32),
            pltpu.VMEM((FIELDS, tile_x, PATCH), F32),
            pltpu.VMEM((32, 256), BF16),
            pltpu.VMEM((2, FIELDS, HALO, PATCH), F32),
            pltpu.VMEM((32, 256), BF16),
            pltpu.VMEM((2, 32, PATCH), BF16),
            pltpu.VMEM((devices, wrows, PATCH), BF16),
            pltpu.VMEM((devices, wrows, PATCH), BF16),
            pltpu.VMEM((devices * jp, FIELDS * 256), BF16),
            pltpu.VMEM((tile_x, PATCH), F32),
            pltpu.VMEM((blocks, PATCH), F32),
            pltpu.VMEM((FIELDS * 256, PATCH), BF16),
            pltpu.VMEM((devices * jp, PATCH), BF16),
            pltpu.VMEM((devices * jp, PATCH), BF16),
            pltpu.VMEM((MARINE * 8, devices * jp), BF16),
            pltpu.VMEM((MARINE, devices * rp), BF16),
            pltpu.VMEM((devices, rp, PATCH), F32),
            pltpu.VMEM((devices, rp, PATCH), F32),
            pltpu.VMEM((MARINE, layers, 8, PATCH), F32),
            pltpu.VMEM((MARINE, layers, 8, PATCH), F32),
            pltpu.VMEM((layers * 8, PATCH), F32),
            pltpu.VMEM((MARINE * 8, PATCH), F32),
            pltpu.VMEM((MARINE * 8, PATCH), F32),
            pltpu.SemaphoreType.DMA((MARINE,)),
            pltpu.SemaphoreType.DMA((MARINE,)),
            pltpu.SemaphoreType.DMA((4,)),
            pltpu.SemaphoreType.DMA((8,)),
            pltpu.SemaphoreType.DMA((8,)),
            pltpu.SemaphoreType.DMA((3,)),
            pltpu.SemaphoreType.DMA((3,)),
        ],
        compiler_params=pltpu.CompilerParams(
            collective_id=0, has_side_effects=True, vmem_limit_bytes=56 * 1024 * 1024
        ),
    )(
        holder, corner, owner.reshape(1, blocks), position.reshape(1, blocks),
        fine, skin, coarse, exchange, jnp.transpose(marine, (1, 0, 2)), op,
    )
    return nest, jnp.transpose(marine_new, (1, 0, 2)), heat


def solution(mesh):
    in_specs = (
        P(None, "gx", "gy"),
        P("gx", "gy"),
        P(None, "gx", "gy"),
        P(),
        P(),
        P(("gx", "gy"), None),
        P(("gx", "gy")),
        P(None, ("gx", "gy")),
        P(None, None, ("gx", "gy")),
        P(),
    )
    out_specs = (P(None, "gx", "gy"), P(None, None, ("gx", "gy")), P("gx", "gy"))
    return jax.shard_map(
        functools.partial(on_device, mesh.shape["gx"], mesh.shape["gy"]),
        mesh=mesh,
        in_specs=in_specs,
        out_specs=out_specs,
        check_vma=False,
    )
```

```python
import functools
import math

import jax
import jax.numpy as jnp
from jax import lax
from jax.experimental import pallas as pl
from jax.experimental.pallas import tpu as pltpu
from jax.sharding import PartitionSpec as P

FIELDS = 4
PATCH = 128
MARINE = 32
STEPS = 4
WCOLS = 32
SLOT_LANE = 18
HALO = 8
DIFFUSE = 0.24
RELAX = 0.3
DRAG = 0.5
F32 = jnp.float32
BF16 = jnp.bfloat16
MESH = pl.DeviceIdType.MESH
NT = (((1,), (1,)), ((), ()))
TN = (((0,), (0,)), ((), ()))


def iota(shape, dim):
    return lax.broadcasted_iota(jnp.int32, shape, dim)


def hot(condition):
    return jnp.where(condition, 1.0, 0.0).astype(BF16)


def dot(a, b):
    return jnp.dot(a, b, preferred_element_type=F32)


def first_parent(first_fine):
    return (4 * first_fine - 11) // 26


def kernel(
    nx, ny, cap, jp, rp, yw, wrows, per,
    holder, corner, owner, position, fine, skin, coarse_far, exchange, marine, op,
    nest_out, marine_out, heat_out,
    coarse, index_row, centre, strips, rows_in, cols_in, corners_in,
    tx1, rx1, pmat, flux_tile, flux_rows, flux_pack, tx2, rx2, amat, qmat, tx3, rx3,
    marine_in, mixed, op_pad, op_column, coarse_rows, forced,
    marine_sem, out_sem, local_sem, halo_send, halo_recv, send_sem, recv_sem,
):
    tile_x, tile_y = fine.shape[1], fine.shape[2]
    blocks = owner.shape[1]
    layers = op.shape[0]
    devices = nx * ny
    ix, iy = lax.axis_index("gx"), lax.axis_index("gy")
    me = ix * ny + iy

    coarse_copy = pltpu.make_async_copy(coarse_far, coarse, local_sem.at[0])
    coarse_copy.start()
    rx3[...] = jnp.zeros(rx3.shape, F32)
    barrier = pltpu.get_barrier_semaphore()

    def greet(t, carry):
        other = lax.rem(me + t, devices)
        pl.semaphore_signal(
            barrier, inc=1, device_id=(lax.div(other, ny), lax.rem(other, ny)), device_id_type=MESH
        )
        return carry

    lax.fori_loop(1, devices, greet, 0)

    def ocean_block(ref, g):
        return ref.at[:, :, pl.ds(pl.multiple_of(g * PATCH, PATCH), PATCH)]

    def fetch(g):
        return pltpu.make_async_copy(
            ocean_block(marine, g), marine_in.at[g, pl.ds(0, layers), pl.ds(0, FIELDS), :], marine_sem.at[g]
        )

    def keep(g):
        return pltpu.make_async_copy(
            mixed.at[g, pl.ds(0, layers), pl.ds(0, FIELDS), :], ocean_block(marine_out, g), out_sem.at[g]
        )

    def each(count, work):
        def one(n, carry):
            work(n)
            return carry

        lax.fori_loop(0, count, one, 0)

    each(MARINE, lambda g: fetch(g).start())

    for f in range(FIELDS):
        centre[f, :, :] = jnp.zeros((tile_x, PATCH), F32)
        centre[f, :, 0:tile_y] = fine[f]
    wide = jnp.concatenate([centre[f].astype(BF16) for f in range(FIELDS)], axis=1)
    r = iota((32, FIELDS * PATCH), 0)
    field_col = ((r & 15) >> 2) * PATCH + (r & 3)
    lane = iota((32, FIELDS * PATCH), 1)
    pick = hot(lane == field_col + jnp.where(r >= 16, tile_y - 4, 0))
    place = hot(lane == field_col + jnp.where(r >= 16, tile_y, PATCH - 4))
    wide = jnp.concatenate([wide, jnp.zeros((256 - tile_x, FIELDS * PATCH), BF16)], axis=0)
    strips[...] = lax.dot_general(pick, wide, NT, preferred_element_type=F32).astype(BF16)

    index_row[...] = jnp.full(index_row.shape, -1, jnp.int32)
    index_row[0:1, 0:blocks] = owner[...]
    index_row[1:2, 0:blocks] = position[...]
    owner_row, pos_row = index_row[0:1, :], index_row[1:2, :]
    k0, k1 = iota((blocks, 256), 0), iota((blocks, 256), 1)
    owner_col = jnp.sum(
        jnp.where(k0 == k1, owner_row.astype(F32), 0.0), axis=1, keepdims=True
    ).astype(jnp.int32)
    same = owner_col == owner_row
    rank_row = jnp.sum(jnp.where(same & (k0 < k1), 1.0, 0.0), axis=0, keepdims=True).astype(jnp.int32)
    rank_col = jnp.sum(jnp.where(same & (k1 < k0), 1.0, 0.0), axis=1, keepdims=True).astype(jnp.int32)

    owners_hot = jnp.where(iota((devices, 256), 0) == owner_row, 1.0, 0.0)
    weighted = (owners_hot * (pos_row + 1).astype(F32)).astype(BF16)
    ranks_hot = hot(iota((PATCH, 256), 0) - SLOT_LANE == rank_row)
    slots = lax.dot_general(weighted, ranks_hot, NT, preferred_element_type=F32)

    coarse_copy.wait()
    cells = coarse.shape[1]
    away = (holder[0] - me) * 65536
    q = iota((cells, yw), 0)
    choose_y = hot(q == iota((cells, yw), 1) + (corner[1] - 1))
    p = iota((wrows, cells), 1) - iota((wrows, cells), 0) - (corner[0] + away)
    choose_x = jnp.concatenate([hot(p == first_parent(a * tile_x - 3)) for a in range(nx)], axis=0)
    windows = []
    for f in range(FIELDS):
        narrow = dot(coarse[f], choose_y).astype(BF16)
        windows.append(dot(choose_x, narrow))
    lane_group = iota((nx * wrows, PATCH), 1) // WCOLS
    lane = iota((wrows, PATCH), 1)
    slot_place = (iota((wrows, PATCH), 0) == 0) & (lane >= SLOT_LANE) & (lane < WCOLS)
    for b in range(ny):
        base = first_parent(b * tile_y - 3) + 1
        piece = jnp.zeros((nx * wrows, PATCH), F32)
        for f in range(FIELDS):
            moved = pltpu.roll(windows[f], (f * WCOLS - base) % yw, 1)[:, 0:PATCH]
            piece = jnp.where(lane_group == f, moved, piece)
        for a in range(nx):
            d = a * ny + b
            part = piece[a * wrows : (a + 1) * wrows]
            tx1[d] = jnp.where(slot_place, slots[d : d + 1, :], part).astype(BF16)

    pl.semaphore_wait(barrier, devices - 1)

    def send(phase, source, target):
        def one(t, carry):
            other = lax.rem(me + t, devices)
            pltpu.make_async_remote_copy(
                src_ref=source(other),
                dst_ref=target,
                send_sem=send_sem.at[phase],
                recv_sem=recv_sem.at[phase],
                device_id=(lax.div(other, ny), lax.rem(other, ny)),
                device_id_type=MESH,
            ).start()
            return carry

        lax.fori_loop(1, devices, one, 0)

    def all_of(ref, sem):
        pltpu.make_async_copy(ref, ref, sem).wait()

    def others(ref, rows):
        return ref.at[pl.ds(0, (devices - 1) * rows)]

    west, east = lax.rem(ix + nx - 1, nx), lax.rem(ix + 1, nx)
    south, north = lax.rem(iy + ny - 1, ny), lax.rem(iy + 1, ny)
    left, right = pl.ds(0, 16), pl.ds(16, 16)
    low, high = pl.ds(0, 128), pl.ds(128, 128)
    halos = [
        (centre.at[:, pl.ds(tile_x - HALO, HALO), :], rows_in.at[0], (east, iy)),
        (centre.at[:, pl.ds(0, HALO), :], rows_in.at[1], (west, iy)),
        (strips.at[right], cols_in.at[left], (ix, north)),
        (strips.at[left], cols_in.at[right], (ix, south)),
        (strips.at[right, high], corners_in.at[0, left], (east, north)),
        (strips.at[left, high], corners_in.at[0, right], (east, south)),
        (strips.at[right, low], corners_in.at[1, left], (west, north)),
        (strips.at[left, low], corners_in.at[1, right], (west, south)),
    ]
    halos = [
        pltpu.make_async_remote_copy(
            src_ref=src, dst_ref=dst, send_sem=halo_send.at[n], recv_sem=halo_recv.at[n],
            device_id=where, device_id_type=MESH,
        )
        for n, (src, dst, where) in enumerate(halos)
    ]
    for copy in halos:
        copy.start()
    send(0, lambda other: tx1.at[other], rx1.at[me])
    own1 = pltpu.make_async_copy(tx1.at[me], rx1.at[me], local_sem.at[1])
    own1.start()

    target = owner_row * jp + rank_row

    chunk = per * jp

    def dispatch_rows(c):
        start = pl.multiple_of(c * chunk, chunk)
        row = iota((chunk, 256), 0) + start
        for f in range(FIELDS):
            pmat[pl.ds(start, chunk), f * 256 : (f + 1) * 256] = hot(row == target + f * cap)

    each(devices // per, dispatch_rows)
    flux_pack[...] = jnp.zeros(flux_pack.shape, BF16)

    deep = marine_in.shape[1]
    op_pad[...] = jnp.zeros(op_pad.shape, F32)
    op_pad[0:layers, 0:layers] = op[...]
    op_high = op_pad[...].astype(BF16).astype(F32)
    op_low = op_pad[...] - op_high
    op_three = op_high + pltpu.roll(op_high, deep, 1) + pltpu.roll(op_low, 2 * deep, 1)
    op_three = op_three.astype(BF16)[:, 0 : 3 * deep]
    pitch = deep * 8
    marine_in[:, layers:, :, :] = jnp.zeros((MARINE, deep - layers, 8, PATCH), F32)
    marine_rows = marine_in.reshape(MARINE * pitch, PATCH)
    mixed_rows = mixed.reshape(MARINE * pitch, PATCH)

    def mix(c):
        for n in range(4):
            fetch(4 * c + n).wait()
        for f in range(FIELDS):
            rows = [pl.ds((4 * c + n) * pitch + f, deep, stride=8) for n in range(4)]
            value = jnp.concatenate([marine_rows[at, :] for at in rows], axis=1)
            m_high = value.astype(BF16)
            m_low = (value - m_high.astype(F32)).astype(BF16)
            value = dot(op_three, jnp.concatenate([m_high, m_low, m_high], axis=0))
            for n, at in enumerate(rows):
                mixed_rows[at, :] = value[:, n * PATCH : (n + 1) * PATCH]

    early = 3
    each(early, mix)

    own1.wait()
    all_of(others(rx1, 1), recv_sem.at[0])
    for copy in halos:
        copy.wait_recv()

    window = lax.fori_loop(
        0, devices, lambda s, total: total + rx1[s].astype(F32), jnp.zeros((wrows, PATCH), F32)
    ).astype(BF16)
    height = tile_x + 2 * HALO
    fx = (iota((height, wrows), 0) + (ix * tile_x - HALO)).astype(F32)
    first_x = (4 * (ix * tile_x - 3) - 11 + 26) // 26 - 1
    at_x = (fx + 0.5) * (2.0 / 13.0) - 0.5 + corner[0].astype(F32)
    px = (iota((height, wrows), 1) + (first_x + corner[0])).astype(F32)
    wx = jnp.maximum(0.0, 1.0 - jnp.abs(at_x - px)).astype(BF16)
    lane_y = iota((PATCH, PATCH), 0)
    lane_y = lane_y - jnp.where(lane_y >= PATCH - 16, PATCH, 0)
    fy = (lane_y + iy * tile_y).astype(F32)
    first_y = (4 * (iy * tile_y - 3) - 11 + 26) // 26 - 1
    at_y = (fy + 0.5) * (2.0 / 13.0) - 0.5 + corner[1].astype(F32)
    py = ((iota((PATCH, PATCH), 1) & (WCOLS - 1)) + (first_y + corner[1])).astype(F32)
    wy = jnp.maximum(0.0, 1.0 - jnp.abs(at_y - py))
    group_y = iota((PATCH, PATCH), 1) // WCOLS

    side = lax.dot_general(cols_in[...], place, TN, preferred_element_type=F32)
    side_low = lax.dot_general(corners_in[0], place, TN, preferred_element_type=F32)
    side_high = lax.dot_general(corners_in[1], place, TN, preferred_element_type=F32)

    gi = iota((height, PATCH), 0) + (ix * tile_x - HALO)
    gj = iota((height, PATCH), 1)
    gj = gj - jnp.where(gj >= PATCH - 16, PATCH, 0) + iy * tile_y
    inside = (gi >= 0) & (gi < nx * tile_x) & (gj >= 0) & (gj < ny * tile_y)
    final = []
    for f in range(FIELDS):
        wy_f = jnp.where(group_y == f, wy, 0.0).astype(BF16)
        partial = lax.dot_general(window, wy_f, NT, preferred_element_type=F32).astype(BF16)
        forcing = dot(wx, partial)
        cut = slice(f * PATCH, (f + 1) * PATCH)
        state = jnp.concatenate(
            [
                rows_in[0, f] + side_low[56:64, cut],
                centre[f] + side[0:tile_x, cut],
                rows_in[1, f] + side_high[0:8, cut],
            ],
            axis=0,
        )
        state = jnp.where(inside, state, 0.0)
        for _ in range(STEPS):
            beside = (
                pltpu.roll(state, 1, 0) + pltpu.roll(state, height - 1, 0)
                + pltpu.roll(state, 1, 1) + pltpu.roll(state, PATCH - 1, 1)
            )
            state = state + DIFFUSE * (beside - 4.0 * state) + RELAX * (forcing - state)
            state = jnp.where(inside, state, 0.0)
        state = state[HALO : HALO + tile_x]
        nest_out[f] = state[:, 0:tile_y]
        final.append(state)

    flux_tile[:, 0:tile_y] = skin[...]
    heat = flux_tile[...]
    u, v, ta, qa = final
    drag = DRAG * jnp.sqrt(1.0 + u * u + v * v)
    lane = iota((tile_x // 4, PATCH), 1)
    for f, flux in enumerate((drag * (ta - heat), drag * (qa - 0.5 * heat), drag * u, drag * v)):
        flux_tile[...] = flux
        f0, f1, f2, f3 = [flux_tile[pl.ds(n, tile_x // 4, stride=4), :] for n in range(4)]
        f1, f2 = pltpu.roll(f1, 96, 1), pltpu.roll(f2, 64, 1)
        flux_rows[pl.ds(0, blocks // 3, stride=3), :] = jnp.where(lane < 96, f0, f1)
        flux_rows[pl.ds(1, blocks // 3, stride=3), :] = jnp.where(lane < 64, f1, f2)
        flux_rows[pl.ds(2, blocks // 3, stride=3), :] = jnp.where(lane < 32, f2, pltpu.roll(f3, 32, 1))
        flux_pack[f * 256 : f * 256 + blocks, :] = flux_rows[...].astype(BF16)

    def part(ref, device, rows):
        return ref.at[pl.ds(pl.multiple_of(device * rows, 16), rows)]

    def flux_to(other):
        return pltpu.make_async_remote_copy(
            src_ref=part(tx2, other, jp),
            dst_ref=part(rx2, me, jp),
            send_sem=send_sem.at[1],
            recv_sem=recv_sem.at[1],
            device_id=(lax.div(other, ny), lax.rem(other, ny)),
            device_id_type=MESH,
        )

    def dispatch(c):
        turn = lax.rem(c + lax.div(me, per), devices // per)
        rows = pl.ds(pl.multiple_of(turn * chunk, chunk), chunk)
        tx2[rows, :] = dot(pmat[rows, :], flux_pack[...]).astype(BF16)
        for n in range(per):
            other = turn * per + n

            @pl.when(other != me)
            def _():
                flux_to(other).start()

    each(devices // per, dispatch)
    own2 = pltpu.make_async_copy(part(tx2, me, jp), part(rx2, me, jp), local_sem.at[2])
    own2.start()

    got = rx1[:, 0:16, :].astype(F32)[:, 0, :].astype(BF16)

    def spread_slots(pitch, fields):
        period = math.lcm(pitch, PATCH)
        a, b = iota((PATCH, period), 0) - SLOT_LANE, iota((PATCH, period), 1)
        rank = b - pitch * sum([jnp.where(b >= n * pitch, 1, 0) for n in range(1, period // pitch)])
        inner = sum([jnp.where(rank >= f * cap, 1, 0) for f in range(1, fields + 1)])
        tiled = dot(got, hot((a == rank - inner * cap) & (a >= 0) & (inner < fields)))
        tiled = jnp.where(tiled > 0.5, tiled * 8.0 + inner[0:1].astype(F32), 0.0)
        tiled = jnp.concatenate([tiled] * (devices * pitch // period), axis=1)
        s, l = iota(tiled.shape, 0), iota(tiled.shape, 1)
        mine = (l >= s * pitch) & (l < (s + 1) * pitch)
        return jnp.sum(jnp.where(mine, tiled, 0.0), axis=0, keepdims=True).astype(jnp.int32) - 8

    each(MARINE // 4 - early, lambda c: mix(c + early))
    column = jnp.broadcast_to(op[:, 0:1], (layers, PATCH))
    for f in range(8):
        op_column[pl.ds(f, layers, stride=8), :] = column
    coarse_rows[...] = jnp.zeros(coarse_rows.shape, F32)
    for g in range(MARINE):
        coarse_rows[g * 8 : g * 8 + FIELDS, :] = exchange[:, g * PATCH : (g + 1) * PATCH]
    amat[...] = hot(iota((MARINE * 8, devices * jp), 0) == spread_slots(jp, FIELDS))
    count = jnp.sum(amat[...].astype(F32), axis=1, keepdims=True)
    qmat[...] = hot(iota((MARINE, devices * rp), 0) * 8 == spread_slots(rp, 1))
    least = jnp.maximum(count, 1.0)
    empty = jnp.where(count == 0.0, coarse_rows[...], 0.0)
    skin_base = mixed_rows[pl.ds(0, MARINE, stride=pitch), :]

    own2.wait()
    all_of(others(rx2, jp), recv_sem.at[1])
    forced[...] = (dot(amat[...], rx2[...]) + empty) / least
    new_skin = skin_base + op[0:1, 0:1] * forced[pl.ds(0, MARINE, stride=8), :]

    def select(matrix, value, dims):
        high = value.astype(BF16)
        low = (value - high.astype(F32)).astype(BF16)
        both = lax.dot_general(
            matrix, jnp.concatenate([high, low], axis=1), dims, preferred_element_type=F32
        )
        return both[:, 0:PATCH] + both[:, PATCH:]

    tx3[...] = select(qmat[...], new_skin, TN).reshape(tx3.shape)
    send(2, lambda other: tx3.at[other, pl.ds(0, cap)], rx3.at[me, pl.ds(0, cap)])
    own3 = pltpu.make_async_copy(tx3.at[me, pl.ds(0, cap)], rx3.at[me, pl.ds(0, cap)], local_sem.at[3])
    own3.start()

    column = op_column[...].reshape(layers, 8, PATCH)

    def force(g):
        mixed[g, 0:layers] = mixed[g, 0:layers] + column * forced[pl.ds(pl.multiple_of(g * 8, 8), 8), :][None]
        keep(g).start()

    each(MARINE, force)
    where_from = hot(iota((blocks, devices * rp), 1) == owner_col * rp + rank_col)
    for copy in halos:
        copy.wait_send()
    all_of(others(tx1, 1), send_sem.at[0])
    all_of(others(tx2, jp), send_sem.at[1])
    own3.wait()
    all_of(rx3.at[pl.ds(0, devices - 1), pl.ds(0, cap)], recv_sem.at[2])
    flux_rows[...] = select(where_from, rx3[...].reshape(devices * rp, PATCH), (((1,), (0,)), ((), ())))
    h0, h1, h2 = [flux_rows[pl.ds(n, blocks // 3, stride=3), :] for n in range(3)]
    h1 = pltpu.roll(h1, 64, 1)
    quarter = tile_x // 4
    flux_tile[pl.ds(0, quarter, stride=4), :] = h0
    flux_tile[pl.ds(1, quarter, stride=4), :] = jnp.where(
        lane < 32, pltpu.roll(h0, 32, 1), pltpu.roll(h1, 96, 1)
    )
    flux_tile[pl.ds(2, quarter, stride=4), :] = jnp.where(lane < 64, h1, pltpu.roll(h2, 64, 1))
    flux_tile[pl.ds(3, quarter, stride=4), :] = pltpu.roll(h2, 96, 1)
    heat_out[...] = flux_tile[:, 0:tile_y]
    all_of(tx3.at[pl.ds(0, devices - 1), pl.ds(0, cap)], send_sem.at[2])
    each(MARINE, lambda g: keep(g).wait())


def on_device(nx, ny, fine, skin, coarse, holder, corner, owner, position, exchange, marine, op):
    devices = nx * ny
    tile_x, tile_y = fine.shape[1:]
    blocks = tile_x * tile_y // PATCH
    cap = max(2, (2 * blocks + devices - 1) // devices)
    jp = -(-FIELDS * cap // 16) * 16
    rp = -(-cap // 16) * 16
    spans = [
        first_parent(min((a + 1) * tile_x + 2, nx * tile_x - 1)) - first_parent(a * tile_x - 3) + 2
        for a in range(nx)
    ]
    wrows = -(-max(spans) // 16) * 16
    per = 2 ** int(math.log2(256 // jp))
    last = first_parent((ny - 1) * tile_y - 3) + 1 + 18
    yw = -(-last // PATCH) * PATCH
    layers, cells = marine.shape[1:]
    deep = -(-layers // 16) * 16
    vmem = pl.BlockSpec(memory_space=pltpu.VMEM)
    smem = pl.BlockSpec(memory_space=pltpu.SMEM)
    anywhere = pl.BlockSpec(memory_space=pl.ANY)
    nest, marine_new, heat = pl.pallas_call(
        functools.partial(kernel, nx, ny, cap, jp, rp, yw, wrows, per),
        out_shape=(
            jax.ShapeDtypeStruct(fine.shape, F32),
            jax.ShapeDtypeStruct((layers, FIELDS, cells), F32),
            jax.ShapeDtypeStruct(skin.shape, F32),
        ),
        in_specs=[smem, smem, vmem, vmem, vmem, vmem, anywhere, vmem, anywhere, vmem],
        out_specs=(vmem, anywhere, vmem),
        scratch_shapes=[
            pltpu.VMEM(coarse.shape, BF16),
            pltpu.VMEM((8, 256), jnp.int32),
            pltpu.VMEM((FIELDS, tile_x, PATCH), F32),
            pltpu.VMEM((32, 256), BF16),
            pltpu.VMEM((2, FIELDS, HALO, PATCH), F32),
            pltpu.VMEM((32, 256), BF16),
            pltpu.VMEM((2, 32, PATCH), BF16),
            pltpu.VMEM((devices, wrows, PATCH), BF16),
            pltpu.VMEM((devices, wrows, PATCH), BF16),
            pltpu.VMEM((devices * jp, FIELDS * 256), BF16),
            pltpu.VMEM((tile_x, PATCH), F32),
            pltpu.VMEM((blocks, PATCH), F32),
            pltpu.VMEM((FIELDS * 256, PATCH), BF16),
            pltpu.VMEM((devices * jp, PATCH), BF16),
            pltpu.VMEM((devices * jp, PATCH), BF16),
            pltpu.VMEM((MARINE * 8, devices * jp), BF16),
            pltpu.VMEM((MARINE, devices * rp), BF16),
            pltpu.VMEM((devices, rp, PATCH), F32),
            pltpu.VMEM((devices, rp, PATCH), F32),
            pltpu.VMEM((MARINE, deep, 8, PATCH), F32),
            pltpu.VMEM((MARINE, deep, 8, PATCH), F32),
            pltpu.VMEM((deep, 256), F32),
            pltpu.VMEM((layers * 8, PATCH), F32),
            pltpu.VMEM((MARINE * 8, PATCH), F32),
            pltpu.VMEM((MARINE * 8, PATCH), F32),
            pltpu.SemaphoreType.DMA((MARINE,)),
            pltpu.SemaphoreType.DMA((MARINE,)),
            pltpu.SemaphoreType.DMA((4,)),
            pltpu.SemaphoreType.DMA((8,)),
            pltpu.SemaphoreType.DMA((8,)),
            pltpu.SemaphoreType.DMA((3,)),
            pltpu.SemaphoreType.DMA((3,)),
        ],
        compiler_params=pltpu.CompilerParams(
            collective_id=0, has_side_effects=True, vmem_limit_bytes=32 * 1024 * 1024
        ),
    )(
        holder, corner, owner.reshape(1, blocks), position.reshape(1, blocks),
        fine, skin, coarse, exchange, jnp.transpose(marine, (1, 0, 2)), op,
    )
    return nest, jnp.transpose(marine_new, (1, 0, 2)), heat


def solution(mesh):
    in_specs = (
        P(None, "gx", "gy"),
        P("gx", "gy"),
        P(None, "gx", "gy"),
        P(),
        P(),
        P(("gx", "gy"), None),
        P(("gx", "gy")),
        P(None, ("gx", "gy")),
        P(None, None, ("gx", "gy")),
        P(),
    )
    out_specs = (P(None, "gx", "gy"), P(None, None, ("gx", "gy")), P("gx", "gy"))
    return jax.shard_map(
        functools.partial(on_device, mesh.shape["gx"], mesh.shape["gy"]),
        mesh=mesh,
        in_specs=in_specs,
        out_specs=out_specs,
        check_vma=False,
    )
```

```python
import functools
import math

import jax
import jax.numpy as jnp
from jax import lax
from jax.experimental import pallas as pl
from jax.experimental.pallas import tpu as pltpu
from jax.sharding import PartitionSpec as P

FIELDS = 4
PATCH = 128
MARINE = 32
STEPS = 4
WCOLS = 32
SLOT_LANE = 18
HALO = 8
DIFFUSE = 0.24
RELAX = 0.3
DRAG = 0.5
F32 = jnp.float32
BF16 = jnp.bfloat16
MESH = pl.DeviceIdType.MESH
NT = (((1,), (1,)), ((), ()))
TN = (((0,), (0,)), ((), ()))


def iota(shape, dim):
    return lax.broadcasted_iota(jnp.int32, shape, dim)


def hot(condition):
    return jnp.where(condition, 1.0, 0.0).astype(BF16)


def dot(a, b):
    return jnp.dot(a, b, preferred_element_type=F32)


def first_parent(first_fine):
    return (4 * first_fine - 11) // 26


def kernel(
    nx, ny, cap, jp, rp, yw, wrows, per,
    holder, corner, owner, position, fine_far, skin_far, coarse_far, exchange_far, marine, op_far,
    nest_out, marine_out, forced_out, heat_out,
    fine, skin, coarse, exchange, op, nest, index_row, centre, strips, rows_in, cols_in, corners_in,
    tx1, rx1, pmat, flux_tile, flux_rows, flux_pack, tx2, rx2, amat, qmat, tx3, rx3,
    marine_in, mixed, op_pad, coarse_rows, forced,
    in_sem, marine_sem, out_sem, nest_sem, local_sem, halo_send, halo_recv, send_sem, recv_sem,
):
    tile_x, tile_y = fine.shape[1], fine.shape[2]
    blocks = owner.shape[1]
    layers = op.shape[0]
    devices = nx * ny
    ix, iy = lax.axis_index("gx"), lax.axis_index("gy")
    me = ix * ny + iy

    arrays = [(coarse_far, coarse), (fine_far, fine), (skin_far, skin), (exchange_far, exchange), (op_far, op)]
    arrays = [pltpu.make_async_copy(far, near, in_sem.at[n]) for n, (far, near) in enumerate(arrays)]
    for copy in arrays:
        copy.start()
    coarse_copy, fine_copy, skin_copy, exchange_copy, op_copy = arrays

    def each(count, work):
        def one(n, carry):
            work(n)
            return carry

        lax.fori_loop(0, count, one, 0)

    power = devices & (devices - 1) == 0 and ny & (ny - 1) == 0 and devices >= 8

    def place_of(device):
        if power:
            return (device >> (ny.bit_length() - 1), device & (ny - 1))
        return (lax.div(device, ny), lax.rem(device, ny))

    def to_others(work):
        if not power:
            each(devices - 1, lambda n: work(lax.rem(me + 1 + n, devices)))
            return
        half = devices // 2

        def far(n, bit):
            return me ^ (((n >> 2) << 3) | bit | (n & 3))

        each(half, lambda n: work(far(n, 4)))
        each(half - 1, lambda n: work(far(n + 1, 0)))

    rx3[...] = jnp.zeros(rx3.shape, F32)
    barrier = pltpu.get_barrier_semaphore()
    to_others(
        lambda other: pl.semaphore_signal(
            barrier, inc=1, device_id=place_of(other), device_id_type=MESH
        )
    )
    def ocean_block(ref, g):
        return ref.at[:, :, pl.ds(pl.multiple_of(g * PATCH, PATCH), PATCH)]

    def fetch(g):
        return pltpu.make_async_copy(
            ocean_block(marine, g), marine_in.at[g, pl.ds(0, layers), pl.ds(0, FIELDS), :], marine_sem.at[g]
        )

    def keep(g):
        return pltpu.make_async_copy(
            mixed.at[g, pl.ds(0, layers), pl.ds(0, FIELDS), :], ocean_block(marine_out, g), out_sem.at[g]
        )

    each(MARINE, lambda g: fetch(g).start())

    fine_copy.wait()
    for f in range(FIELDS):
        centre[f, :, :] = jnp.zeros((tile_x, PATCH), F32)
        centre[f, :, 0:tile_y] = fine[f]
    wide = jnp.concatenate([centre[f].astype(BF16) for f in range(FIELDS)], axis=1)
    r = iota((32, FIELDS * PATCH), 0)
    field_col = ((r & 15) >> 2) * PATCH + (r & 3)
    lane = iota((32, FIELDS * PATCH), 1)
    pick = hot(lane == field_col + jnp.where(r >= 16, tile_y - 4, 0))
    place = hot(lane == field_col + jnp.where(r >= 16, tile_y, PATCH - 4))
    wide = jnp.concatenate([wide, jnp.zeros((256 - tile_x, FIELDS * PATCH), BF16)], axis=0)
    strips[...] = lax.dot_general(pick, wide, NT, preferred_element_type=F32).astype(BF16)

    index_row[...] = jnp.full(index_row.shape, -1, jnp.int32)
    index_row[0:1, 0:blocks] = owner[...]
    index_row[1:2, 0:blocks] = position[...]
    owner_row, pos_row = index_row[0:1, :], index_row[1:2, :]
    k0, k1 = iota((blocks, 256), 0), iota((blocks, 256), 1)
    owner_col = jnp.sum(
        jnp.where(k0 == k1, owner_row.astype(F32), 0.0), axis=1, keepdims=True
    ).astype(jnp.int32)
    same = owner_col == owner_row
    rank_row = jnp.sum(jnp.where(same & (k0 < k1), 1.0, 0.0), axis=0, keepdims=True).astype(jnp.int32)
    rank_col = jnp.sum(jnp.where(same & (k1 < k0), 1.0, 0.0), axis=1, keepdims=True).astype(jnp.int32)

    owners_hot = jnp.where(iota((devices, 256), 0) == owner_row, 1.0, 0.0)
    weighted = (owners_hot * (pos_row + 1).astype(F32)).astype(BF16)
    ranks_hot = hot(iota((PATCH, 256), 0) - SLOT_LANE == rank_row)
    slots = lax.dot_general(weighted, ranks_hot, NT, preferred_element_type=F32)

    coarse_copy.wait()
    cells = coarse.shape[1]
    away = (holder[0] - me) * 65536
    q = iota((cells, yw), 0)
    choose_y = hot(q == iota((cells, yw), 1) + (corner[1] - 1))
    p = iota((wrows, cells), 1) - iota((wrows, cells), 0) - (corner[0] + away)
    choose_x = jnp.concatenate([hot(p == first_parent(a * tile_x - 3)) for a in range(nx)], axis=0)
    windows = []
    for f in range(FIELDS):
        narrow = dot(coarse[f], choose_y).astype(BF16)
        windows.append(dot(choose_x, narrow))
    lane_group = iota((nx * wrows, PATCH), 1) // WCOLS
    lane = iota((wrows, PATCH), 1)
    slot_place = (iota((wrows, PATCH), 0) == 0) & (lane >= SLOT_LANE) & (lane < WCOLS)
    for b in range(ny):
        base = first_parent(b * tile_y - 3) + 1
        piece = jnp.zeros((nx * wrows, PATCH), F32)
        for f in range(FIELDS):
            moved = pltpu.roll(windows[f], (f * WCOLS - base) % yw, 1)[:, 0:PATCH]
            piece = jnp.where(lane_group == f, moved, piece)
        for a in range(nx):
            d = a * ny + b
            part = piece[a * wrows : (a + 1) * wrows]
            tx1[d] = jnp.where(slot_place, slots[d : d + 1, :], part).astype(BF16)

    pl.semaphore_wait(barrier, devices - 1)

    def send(phase, source, target):
        to_others(
            lambda other: pltpu.make_async_remote_copy(
                src_ref=source(other),
                dst_ref=target,
                send_sem=send_sem.at[phase],
                recv_sem=recv_sem.at[phase],
                device_id=place_of(other),
                device_id_type=MESH,
            ).start()
        )

    def all_of(ref, sem):
        pltpu.make_async_copy(ref, ref, sem).wait()

    def others(ref, rows):
        return ref.at[pl.ds(0, (devices - 1) * rows)]

    west, east = lax.rem(ix + nx - 1, nx), lax.rem(ix + 1, nx)
    south, north = lax.rem(iy + ny - 1, ny), lax.rem(iy + 1, ny)
    left, right = pl.ds(0, 16), pl.ds(16, 16)
    low, high = pl.ds(0, 128), pl.ds(128, 128)
    halos = [
        (centre.at[:, pl.ds(tile_x - HALO, HALO), :], rows_in.at[0], (east, iy)),
        (centre.at[:, pl.ds(0, HALO), :], rows_in.at[1], (west, iy)),
        (strips.at[right], cols_in.at[left], (ix, north)),
        (strips.at[left], cols_in.at[right], (ix, south)),
        (strips.at[right, high], corners_in.at[0, left], (east, north)),
        (strips.at[left, high], corners_in.at[0, right], (east, south)),
        (strips.at[right, low], corners_in.at[1, left], (west, north)),
        (strips.at[left, low], corners_in.at[1, right], (west, south)),
    ]
    halos = [
        pltpu.make_async_remote_copy(
            src_ref=src, dst_ref=dst, send_sem=halo_send.at[n], recv_sem=halo_recv.at[n],
            device_id=where, device_id_type=MESH,
        )
        for n, (src, dst, where) in enumerate(halos)
    ]
    for copy in halos:
        copy.start()
    send(0, lambda other: tx1.at[other], rx1.at[me])
    own1 = pltpu.make_async_copy(tx1.at[me], rx1.at[me], local_sem.at[1])
    own1.start()

    target = owner_row * jp + rank_row

    chunk = per * jp

    def dispatch_rows(c):
        start = pl.multiple_of(c * chunk, chunk)
        row = iota((chunk, 256), 0) + start
        for f in range(FIELDS):
            pmat[pl.ds(start, chunk), f * 256 : (f + 1) * 256] = hot(row == target + f * cap)

    each(devices // per, dispatch_rows)
    flux_pack[...] = jnp.zeros(flux_pack.shape, BF16)

    deep = marine_in.shape[1]
    op_copy.wait()
    op_pad[...] = jnp.zeros(op_pad.shape, F32)
    op_pad[0:layers, 0:layers] = op[...]
    op_high = op_pad[...].astype(BF16).astype(F32)
    op_low = op_pad[...] - op_high
    op_three = op_high + pltpu.roll(op_high, deep, 1) + pltpu.roll(op_low, 2 * deep, 1)
    op_three = op_three.astype(BF16)[:, 0 : 3 * deep]
    pitch = deep * 8
    marine_in[:, layers:, :, :] = jnp.zeros((MARINE, deep - layers, 8, PATCH), F32)
    marine_rows = marine_in.reshape(MARINE * pitch, PATCH)
    mixed_rows = mixed.reshape(MARINE * pitch, PATCH)

    def mix(c):
        for n in range(4):
            fetch(4 * c + n).wait()
        for f in range(FIELDS):
            rows = [pl.ds((4 * c + n) * pitch + f, deep, stride=8) for n in range(4)]
            value = jnp.concatenate([marine_rows[at, :] for at in rows], axis=1)
            m_high = value.astype(BF16)
            m_low = (value - m_high.astype(F32)).astype(BF16)
            value = dot(op_three, jnp.concatenate([m_high, m_low, m_high], axis=0))
            for n, at in enumerate(rows):
                mixed_rows[at, :] = value[:, n * PATCH : (n + 1) * PATCH]
        for n in range(4):
            keep(4 * c + n).start()

    early = 3
    each(early, mix)

    own1.wait()
    all_of(others(rx1, 1), recv_sem.at[0])
    for copy in halos:
        copy.wait_recv()

    window = lax.fori_loop(
        0, devices, lambda s, total: total + rx1[s].astype(F32), jnp.zeros((wrows, PATCH), F32)
    ).astype(BF16)
    height = tile_x + 2 * HALO
    fx = (iota((height, wrows), 0) + (ix * tile_x - HALO)).astype(F32)
    first_x = (4 * (ix * tile_x - 3) - 11 + 26) // 26 - 1
    at_x = (fx + 0.5) * (2.0 / 13.0) - 0.5 + corner[0].astype(F32)
    px = (iota((height, wrows), 1) + (first_x + corner[0])).astype(F32)
    wx = jnp.maximum(0.0, 1.0 - jnp.abs(at_x - px)).astype(BF16)
    lane_y = iota((PATCH, PATCH), 0)
    lane_y = lane_y - jnp.where(lane_y >= PATCH - 16, PATCH, 0)
    fy = (lane_y + iy * tile_y).astype(F32)
    first_y = (4 * (iy * tile_y - 3) - 11 + 26) // 26 - 1
    at_y = (fy + 0.5) * (2.0 / 13.0) - 0.5 + corner[1].astype(F32)
    py = ((iota((PATCH, PATCH), 1) & (WCOLS - 1)) + (first_y + corner[1])).astype(F32)
    wy = jnp.maximum(0.0, 1.0 - jnp.abs(at_y - py))
    group_y = iota((PATCH, PATCH), 1) // WCOLS

    side = lax.dot_general(cols_in[...], place, TN, preferred_element_type=F32)
    side_low = lax.dot_general(corners_in[0], place, TN, preferred_element_type=F32)
    side_high = lax.dot_general(corners_in[1], place, TN, preferred_element_type=F32)

    gi = iota((height, PATCH), 0) + (ix * tile_x - HALO)
    gj = iota((height, PATCH), 1)
    gj = gj - jnp.where(gj >= PATCH - 16, PATCH, 0) + iy * tile_y
    inside = (gi >= 0) & (gi < nx * tile_x) & (gj >= 0) & (gj < ny * tile_y)
    final = []
    for f in range(FIELDS):
        wy_f = jnp.where(group_y == f, wy, 0.0).astype(BF16)
        partial = lax.dot_general(window, wy_f, NT, preferred_element_type=F32).astype(BF16)
        forcing = dot(wx, partial)
        cut = slice(f * PATCH, (f + 1) * PATCH)
        state = jnp.concatenate(
            [
                rows_in[0, f] + side_low[56:64, cut],
                centre[f] + side[0:tile_x, cut],
                rows_in[1, f] + side_high[0:8, cut],
            ],
            axis=0,
        )
        state = jnp.where(inside, state, 0.0)
        for _ in range(STEPS):
            beside = (
                pltpu.roll(state, 1, 0) + pltpu.roll(state, height - 1, 0)
                + pltpu.roll(state, 1, 1) + pltpu.roll(state, PATCH - 1, 1)
            )
            state = state + DIFFUSE * (beside - 4.0 * state) + RELAX * (forcing - state)
            state = jnp.where(inside, state, 0.0)
        state = state[HALO : HALO + tile_x]
        nest[f] = state
        final.append(state)

    nest_copy = pltpu.make_async_copy(nest, nest_out, nest_sem)
    nest_copy.start()
    skin_copy.wait()
    flux_tile[:, 0:tile_y] = skin[...]
    heat = flux_tile[...]
    u, v, ta, qa = final
    drag = DRAG * jnp.sqrt(1.0 + u * u + v * v)
    lane = iota((tile_x // 4, PATCH), 1)
    for f, flux in enumerate((drag * (ta - heat), drag * (qa - 0.5 * heat), drag * u, drag * v)):
        flux_tile[...] = flux
        f0, f1, f2, f3 = [flux_tile[pl.ds(n, tile_x // 4, stride=4), :] for n in range(4)]
        f1, f2 = pltpu.roll(f1, 96, 1), pltpu.roll(f2, 64, 1)
        flux_rows[pl.ds(0, blocks // 3, stride=3), :] = jnp.where(lane < 96, f0, f1)
        flux_rows[pl.ds(1, blocks // 3, stride=3), :] = jnp.where(lane < 64, f1, f2)
        flux_rows[pl.ds(2, blocks // 3, stride=3), :] = jnp.where(lane < 32, f2, pltpu.roll(f3, 32, 1))
        flux_pack[f * 256 : f * 256 + blocks, :] = flux_rows[...].astype(BF16)

    def part(ref, device, rows):
        return ref.at[pl.ds(pl.multiple_of(device * rows, 16), rows)]

    def flux_to(other):
        return pltpu.make_async_remote_copy(
            src_ref=part(tx2, other, jp),
            dst_ref=part(rx2, me, jp),
            send_sem=send_sem.at[1],
            recv_sem=recv_sem.at[1],
            device_id=place_of(other),
            device_id_type=MESH,
        )

    turns = devices // per

    def dispatch(c):
        if power:
            half = turns // 2
            late = jnp.where(c >= half, 1, 0)
            turn = (((c - late * half) << 1) | (1 - late)) ^ (me >> (per.bit_length() - 1))
        else:
            turn = lax.rem(c + lax.div(me, per), turns)
        rows = pl.ds(pl.multiple_of(turn * chunk, chunk), chunk)
        tx2[rows, :] = dot(pmat[rows, :], flux_pack[...]).astype(BF16)
        for n in range(per):
            other = turn * per + n

            @pl.when(other != me)
            def _():
                flux_to(other).start()

    each(turns, dispatch)
    own2 = pltpu.make_async_copy(part(tx2, me, jp), part(rx2, me, jp), local_sem.at[2])
    own2.start()

    got = rx1[:, 0:16, :].astype(F32)[:, 0, :].astype(BF16)

    def spread_slots(pitch, fields):
        period = math.lcm(pitch, PATCH)
        a, b = iota((PATCH, period), 0) - SLOT_LANE, iota((PATCH, period), 1)
        rank = b - pitch * sum([jnp.where(b >= n * pitch, 1, 0) for n in range(1, period // pitch)])
        inner = sum([jnp.where(rank >= f * cap, 1, 0) for f in range(1, fields + 1)])
        tiled = dot(got, hot((a == rank - inner * cap) & (a >= 0) & (inner < fields)))
        tiled = jnp.where(tiled > 0.5, tiled * 8.0 + inner[0:1].astype(F32), 0.0)
        tiled = jnp.concatenate([tiled] * (devices * pitch // period), axis=1)
        s, l = iota(tiled.shape, 0), iota(tiled.shape, 1)
        mine = (l >= s * pitch) & (l < (s + 1) * pitch)
        return jnp.sum(jnp.where(mine, tiled, 0.0), axis=0, keepdims=True).astype(jnp.int32) - 8

    each(MARINE // 4 - early, lambda c: mix(c + early))
    exchange_copy.wait()
    coarse_rows[...] = jnp.zeros(coarse_rows.shape, F32)
    for g in range(MARINE):
        coarse_rows[g * 8 : g * 8 + FIELDS, :] = exchange[:, g * PATCH : (g + 1) * PATCH]
    amat[...] = hot(iota((MARINE * 8, devices * jp), 0) == spread_slots(jp, FIELDS))
    count = jnp.sum(amat[...].astype(F32), axis=1, keepdims=True)
    qmat[...] = hot(iota((MARINE, devices * rp), 0) * 8 == spread_slots(rp, 1))
    least = jnp.maximum(count, 1.0)
    empty = jnp.where(count == 0.0, coarse_rows[...], 0.0)
    skin_base = mixed_rows[pl.ds(0, MARINE, stride=pitch), :]

    own2.wait()
    all_of(others(rx2, jp), recv_sem.at[1])
    forced[...] = (dot(amat[...], rx2[...]) + empty) / least
    new_skin = skin_base + op[0:1, 0:1] * forced[pl.ds(0, MARINE, stride=8), :]

    def select(matrix, value, dims):
        high = value.astype(BF16)
        low = (value - high.astype(F32)).astype(BF16)
        both = lax.dot_general(
            matrix, jnp.concatenate([high, low], axis=1), dims, preferred_element_type=F32
        )
        return both[:, 0:PATCH] + both[:, PATCH:]

    tx3[...] = select(qmat[...], new_skin, TN).reshape(tx3.shape)
    send(2, lambda other: tx3.at[other, pl.ds(0, cap)], rx3.at[me, pl.ds(0, cap)])
    own3 = pltpu.make_async_copy(tx3.at[me, pl.ds(0, cap)], rx3.at[me, pl.ds(0, cap)], local_sem.at[3])
    own3.start()

    for g in range(MARINE):
        forced_out[:, g * PATCH : (g + 1) * PATCH] = forced[g * 8 : g * 8 + FIELDS, :]
    where_from = hot(iota((blocks, devices * rp), 1) == owner_col * rp + rank_col)
    for copy in halos:
        copy.wait_send()
    all_of(others(tx1, 1), send_sem.at[0])
    all_of(others(tx2, jp), send_sem.at[1])
    own3.wait()
    all_of(rx3.at[pl.ds(0, devices - 1), pl.ds(0, cap)], recv_sem.at[2])
    flux_rows[...] = select(where_from, rx3[...].reshape(devices * rp, PATCH), (((1,), (0,)), ((), ())))
    h0, h1, h2 = [flux_rows[pl.ds(n, blocks // 3, stride=3), :] for n in range(3)]
    h1 = pltpu.roll(h1, 64, 1)
    quarter = tile_x // 4
    flux_tile[pl.ds(0, quarter, stride=4), :] = h0
    flux_tile[pl.ds(1, quarter, stride=4), :] = jnp.where(
        lane < 32, pltpu.roll(h0, 32, 1), pltpu.roll(h1, 96, 1)
    )
    flux_tile[pl.ds(2, quarter, stride=4), :] = jnp.where(lane < 64, h1, pltpu.roll(h2, 64, 1))
    flux_tile[pl.ds(3, quarter, stride=4), :] = pltpu.roll(h2, 96, 1)
    heat_out[...] = flux_tile[...]
    nest_copy.wait()
    all_of(tx3.at[pl.ds(0, devices - 1), pl.ds(0, cap)], send_sem.at[2])
    each(MARINE, lambda g: keep(g).wait())


def on_device(nx, ny, fine, skin, coarse, holder, corner, owner, position, exchange, marine, op):
    devices = nx * ny
    tile_x, tile_y = fine.shape[1:]
    blocks = tile_x * tile_y // PATCH
    cap = max(2, (2 * blocks + devices - 1) // devices)
    jp = -(-FIELDS * cap // 16) * 16
    rp = -(-cap // 16) * 16
    spans = [
        first_parent(min((a + 1) * tile_x + 2, nx * tile_x - 1)) - first_parent(a * tile_x - 3) + 2
        for a in range(nx)
    ]
    wrows = -(-max(spans) // 16) * 16
    per = 2 ** int(math.log2(256 // jp))
    last = first_parent((ny - 1) * tile_y - 3) + 1 + 18
    yw = -(-last // PATCH) * PATCH
    layers, cells = marine.shape[1:]
    deep = -(-layers // 16) * 16
    vmem = pl.BlockSpec(memory_space=pltpu.VMEM)
    smem = pl.BlockSpec(memory_space=pltpu.SMEM)
    anywhere = pl.BlockSpec(memory_space=pl.ANY)
    nest, mixed, forced, heat = pl.pallas_call(
        functools.partial(kernel, nx, ny, cap, jp, rp, yw, wrows, per),
        out_shape=(
            jax.ShapeDtypeStruct((FIELDS, tile_x, PATCH), F32),
            jax.ShapeDtypeStruct((layers, FIELDS, cells), F32),
            jax.ShapeDtypeStruct((FIELDS, cells), F32),
            jax.ShapeDtypeStruct((tile_x, PATCH), F32),
        ),
        in_specs=[smem, smem, vmem, vmem] + [anywhere] * 6,
        out_specs=(anywhere, anywhere, vmem, vmem),
        scratch_shapes=[
            pltpu.VMEM(fine.shape, F32),
            pltpu.VMEM(skin.shape, F32),
            pltpu.VMEM(coarse.shape, BF16),
            pltpu.VMEM(exchange.shape, F32),
            pltpu.VMEM(op.shape, F32),
            pltpu.VMEM((FIELDS, tile_x, PATCH), F32),
            pltpu.VMEM((8, 256), jnp.int32),
            pltpu.VMEM((FIELDS, tile_x, PATCH), F32),
            pltpu.VMEM((32, 256), BF16),
            pltpu.VMEM((2, FIELDS, HALO, PATCH), F32),
            pltpu.VMEM((32, 256), BF16),
            pltpu.VMEM((2, 32, PATCH), BF16),
            pltpu.VMEM((devices, wrows, PATCH), BF16),
            pltpu.VMEM((devices, wrows, PATCH), BF16),
            pltpu.VMEM((devices * jp, FIELDS * 256), BF16),
            pltpu.VMEM((tile_x, PATCH), F32),
            pltpu.VMEM((blocks, PATCH), F32),
            pltpu.VMEM((FIELDS * 256, PATCH), BF16),
            pltpu.VMEM((devices * jp, PATCH), BF16),
            pltpu.VMEM((devices * jp, PATCH), BF16),
            pltpu.VMEM((MARINE * 8, devices * jp), BF16),
            pltpu.VMEM((MARINE, devices * rp), BF16),
            pltpu.VMEM((devices, rp, PATCH), F32),
            pltpu.VMEM((devices, rp, PATCH), F32),
            pltpu.VMEM((MARINE, deep, 8, PATCH), F32),
            pltpu.VMEM((MARINE, deep, 8, PATCH), F32),
            pltpu.VMEM((deep, 256), F32),
            pltpu.VMEM((MARINE * 8, PATCH), F32),
            pltpu.VMEM((MARINE * 8, PATCH), F32),
            pltpu.SemaphoreType.DMA((5,)),
            pltpu.SemaphoreType.DMA((MARINE,)),
            pltpu.SemaphoreType.DMA((MARINE,)),
            pltpu.SemaphoreType.DMA,
            pltpu.SemaphoreType.DMA((4,)),
            pltpu.SemaphoreType.DMA((8,)),
            pltpu.SemaphoreType.DMA((8,)),
            pltpu.SemaphoreType.DMA((3,)),
            pltpu.SemaphoreType.DMA((3,)),
        ],
        compiler_params=pltpu.CompilerParams(
            collective_id=0, has_side_effects=True, vmem_limit_bytes=56 * 1024 * 1024
        ),
    )(
        holder, corner, owner.reshape(1, blocks), position.reshape(1, blocks),
        fine, skin, coarse, exchange, jnp.transpose(marine, (1, 0, 2)), op,
    )
    marine_new = mixed + op[:, 0][:, None, None] * forced[None]
    return nest[:, :, 0:tile_y], jnp.transpose(marine_new, (1, 0, 2)), heat[:, 0:tile_y]


def solution(mesh):
    in_specs = (
        P(None, "gx", "gy"),
        P("gx", "gy"),
        P(None, "gx", "gy"),
        P(),
        P(),
        P(("gx", "gy"), None),
        P(("gx", "gy")),
        P(None, ("gx", "gy")),
        P(None, None, ("gx", "gy")),
        P(),
    )
    out_specs = (P(None, "gx", "gy"), P(None, None, ("gx", "gy")), P("gx", "gy"))
    return jax.shard_map(
        functools.partial(on_device, mesh.shape["gx"], mesh.shape["gy"]),
        mesh=mesh,
        in_specs=in_specs,
        out_specs=out_specs,
        check_vma=False,
    )
```

```python
import functools
import math

import jax
import jax.numpy as jnp
from jax import lax
from jax.experimental import pallas as pl
from jax.experimental.pallas import tpu as pltpu
from jax.sharding import PartitionSpec as P

FIELDS = 4
PATCH = 128
MARINE = 32
STEPS = 4
WCOLS = 32
SLOT_LANE = 18
HALO = 8
DIFFUSE = 0.24
RELAX = 0.3
DRAG = 0.5
F32 = jnp.float32
BF16 = jnp.bfloat16
MESH = pl.DeviceIdType.MESH
NT = (((1,), (1,)), ((), ()))
TN = (((0,), (0,)), ((), ()))


def iota(shape, dim):
    return lax.broadcasted_iota(jnp.int32, shape, dim)


def hot(condition):
    return jnp.where(condition, 1.0, 0.0).astype(BF16)


def dot(a, b):
    return jnp.dot(a, b, preferred_element_type=F32)


def first_parent(first_fine):
    return (4 * first_fine - 11) // 26


def kernel(
    nx, ny, cap, jp, rp, yw, wrows, per,
    holder, corner, owner, position, fine_far, skin_far, coarse_far, exchange_far, marine, op_far,
    nest_out, marine_out, forced_out, heat_out,
    fine, skin, coarse, exchange, op, nest, index_row, centre, strips, rows_in, cols_in, corners_in,
    tx1, rx1, pmat, flux_tile, flux_rows, flux_pack, tx2, rx2, amat, qmat, tx3, rx3,
    marine_in, mixed, op_pad, coarse_rows, forced,
    in_sem, marine_sem, out_sem, nest_sem, local_sem, halo_send, halo_recv, send_sem, recv_sem,
):
    tile_x, tile_y = fine.shape[1], fine.shape[2]
    blocks = owner.shape[1]
    layers = op.shape[0]
    devices = nx * ny
    ix, iy = lax.axis_index("gx"), lax.axis_index("gy")
    me = ix * ny + iy

    arrays = [(coarse_far, coarse), (fine_far, fine), (skin_far, skin), (exchange_far, exchange), (op_far, op)]
    arrays = [pltpu.make_async_copy(far, near, in_sem.at[n]) for n, (far, near) in enumerate(arrays)]
    for copy in arrays:
        copy.start()
    coarse_copy, fine_copy, skin_copy, exchange_copy, op_copy = arrays

    def each(count, work):
        def one(n, carry):
            work(n)
            return carry

        lax.fori_loop(0, count, one, 0)

    power = devices & (devices - 1) == 0 and ny & (ny - 1) == 0 and devices >= 8

    def place_of(device):
        if power:
            return (device >> (ny.bit_length() - 1), device & (ny - 1))
        return (lax.div(device, ny), lax.rem(device, ny))

    def to_others(work):
        if not power:
            each(devices - 1, lambda n: work(lax.rem(me + 1 + n, devices)))
            return

        def nth(n):
            return me ^ (((n & 1) << 2) | ((n >> 1) & 3) | ((n >> 3) << 3))

        each(devices - 1, lambda n: work(nth(n + 1)))

    rx3[...] = jnp.zeros(rx3.shape, F32)
    barrier = pltpu.get_barrier_semaphore()
    to_others(
        lambda other: pl.semaphore_signal(
            barrier, inc=1, device_id=place_of(other), device_id_type=MESH
        )
    )
    def ocean_block(ref, g):
        return ref.at[:, :, pl.ds(pl.multiple_of(g * PATCH, PATCH), PATCH)]

    def fetch(g):
        return pltpu.make_async_copy(
            ocean_block(marine, g), marine_in.at[g, pl.ds(0, layers), pl.ds(0, FIELDS), :], marine_sem.at[g]
        )

    def keep(g):
        return pltpu.make_async_copy(
            mixed.at[g, pl.ds(0, layers), pl.ds(0, FIELDS), :], ocean_block(marine_out, g), out_sem.at[g]
        )

    each(MARINE, lambda g: fetch(g).start())

    fine_copy.wait()
    for f in range(FIELDS):
        centre[f, :, :] = jnp.zeros((tile_x, PATCH), F32)
        centre[f, :, 0:tile_y] = fine[f]
    wide = jnp.concatenate([centre[f].astype(BF16) for f in range(FIELDS)], axis=1)
    r = iota((32, FIELDS * PATCH), 0)
    field_col = ((r & 15) >> 2) * PATCH + (r & 3)
    lane = iota((32, FIELDS * PATCH), 1)
    pick = hot(lane == field_col + jnp.where(r >= 16, tile_y - 4, 0))
    place = hot(lane == field_col + jnp.where(r >= 16, tile_y, PATCH - 4))
    wide = jnp.concatenate([wide, jnp.zeros((256 - tile_x, FIELDS * PATCH), BF16)], axis=0)
    strips[...] = lax.dot_general(pick, wide, NT, preferred_element_type=F32).astype(BF16)

    index_row[...] = jnp.full(index_row.shape, -1, jnp.int32)
    index_row[0:1, 0:blocks] = owner[...]
    index_row[1:2, 0:blocks] = position[...]
    owner_row, pos_row = index_row[0:1, :], index_row[1:2, :]
    k0, k1 = iota((blocks, 256), 0), iota((blocks, 256), 1)
    owner_col = jnp.sum(
        jnp.where(k0 == k1, owner_row.astype(F32), 0.0), axis=1, keepdims=True
    ).astype(jnp.int32)
    same = owner_col == owner_row
    rank_row = jnp.sum(jnp.where(same & (k0 < k1), 1.0, 0.0), axis=0, keepdims=True).astype(jnp.int32)
    rank_col = jnp.sum(jnp.where(same & (k1 < k0), 1.0, 0.0), axis=1, keepdims=True).astype(jnp.int32)

    owners_hot = jnp.where(iota((devices, 256), 0) == owner_row, 1.0, 0.0)
    weighted = (owners_hot * (pos_row + 1).astype(F32)).astype(BF16)
    ranks_hot = hot(iota((PATCH, 256), 0) - SLOT_LANE == rank_row)
    slots = lax.dot_general(weighted, ranks_hot, NT, preferred_element_type=F32)

    coarse_copy.wait()
    cells = coarse.shape[1]
    away = (holder[0] - me) * 65536
    q = iota((cells, yw), 0)
    choose_y = hot(q == iota((cells, yw), 1) + (corner[1] - 1))
    p = iota((wrows, cells), 1) - iota((wrows, cells), 0) - (corner[0] + away)
    choose_x = jnp.concatenate([hot(p == first_parent(a * tile_x - 3)) for a in range(nx)], axis=0)
    windows = []
    for f in range(FIELDS):
        narrow = dot(coarse[f], choose_y).astype(BF16)
        windows.append(dot(choose_x, narrow))
    lane_group = iota((nx * wrows, PATCH), 1) // WCOLS
    lane = iota((wrows, PATCH), 1)
    slot_place = (iota((wrows, PATCH), 0) == 0) & (lane >= SLOT_LANE) & (lane < WCOLS)
    for b in range(ny):
        base = first_parent(b * tile_y - 3) + 1
        piece = jnp.zeros((nx * wrows, PATCH), F32)
        for f in range(FIELDS):
            moved = pltpu.roll(windows[f], (f * WCOLS - base) % yw, 1)[:, 0:PATCH]
            piece = jnp.where(lane_group == f, moved, piece)
        for a in range(nx):
            d = a * ny + b
            part = piece[a * wrows : (a + 1) * wrows]
            tx1[d] = jnp.where(slot_place, slots[d : d + 1, :], part).astype(BF16)

    pl.semaphore_wait(barrier, devices - 1)

    def send(phase, source, target):
        to_others(
            lambda other: pltpu.make_async_remote_copy(
                src_ref=source(other),
                dst_ref=target,
                send_sem=send_sem.at[phase],
                recv_sem=recv_sem.at[phase],
                device_id=place_of(other),
                device_id_type=MESH,
            ).start()
        )

    def all_of(ref, sem):
        pltpu.make_async_copy(ref, ref, sem).wait()

    def others(ref, rows):
        return ref.at[pl.ds(0, (devices - 1) * rows)]

    west, east = lax.rem(ix + nx - 1, nx), lax.rem(ix + 1, nx)
    south, north = lax.rem(iy + ny - 1, ny), lax.rem(iy + 1, ny)
    left, right = pl.ds(0, 16), pl.ds(16, 16)
    low, high = pl.ds(0, 128), pl.ds(128, 128)
    halos = [
        (centre.at[:, pl.ds(tile_x - HALO, HALO), :], rows_in.at[0], (east, iy)),
        (centre.at[:, pl.ds(0, HALO), :], rows_in.at[1], (west, iy)),
        (strips.at[right], cols_in.at[left], (ix, north)),
        (strips.at[left], cols_in.at[right], (ix, south)),
        (strips.at[right, high], corners_in.at[0, left], (east, north)),
        (strips.at[left, high], corners_in.at[0, right], (east, south)),
        (strips.at[right, low], corners_in.at[1, left], (west, north)),
        (strips.at[left, low], corners_in.at[1, right], (west, south)),
    ]
    halos = [
        pltpu.make_async_remote_copy(
            src_ref=src, dst_ref=dst, send_sem=halo_send.at[n], recv_sem=halo_recv.at[n],
            device_id=where, device_id_type=MESH,
        )
        for n, (src, dst, where) in enumerate(halos)
    ]
    for copy in halos:
        copy.start()
    send(0, lambda other: tx1.at[other], rx1.at[me])
    own1 = pltpu.make_async_copy(tx1.at[me], rx1.at[me], local_sem.at[1])
    own1.start()

    target = owner_row * jp + rank_row

    chunk = per * jp

    def dispatch_rows(c):
        start = pl.multiple_of(c * chunk, chunk)
        row = iota((chunk, 256), 0) + start
        for f in range(FIELDS):
            pmat[pl.ds(start, chunk), f * 256 : (f + 1) * 256] = hot(row == target + f * cap)

    each(devices // per, dispatch_rows)
    flux_pack[...] = jnp.zeros(flux_pack.shape, BF16)

    deep = marine_in.shape[1]
    op_copy.wait()
    op_pad[...] = jnp.zeros(op_pad.shape, F32)
    op_pad[0:layers, 0:layers] = op[...]
    op_high = op_pad[...].astype(BF16).astype(F32)
    op_low = op_pad[...] - op_high
    op_three = op_high + pltpu.roll(op_high, deep, 1) + pltpu.roll(op_low, 2 * deep, 1)
    op_three = op_three.astype(BF16)[:, 0 : 3 * deep]
    pitch = deep * 8
    marine_in[:, layers:, :, :] = jnp.zeros((MARINE, deep - layers, 8, PATCH), F32)
    marine_rows = marine_in.reshape(MARINE * pitch, PATCH)
    mixed_rows = mixed.reshape(MARINE * pitch, PATCH)

    def mix(c):
        for n in range(4):
            fetch(4 * c + n).wait()
        for f in range(FIELDS):
            rows = [pl.ds((4 * c + n) * pitch + f, deep, stride=8) for n in range(4)]
            value = jnp.concatenate([marine_rows[at, :] for at in rows], axis=1)
            m_high = value.astype(BF16)
            m_low = (value - m_high.astype(F32)).astype(BF16)
            value = dot(op_three, jnp.concatenate([m_high, m_low, m_high], axis=0))
            for n, at in enumerate(rows):
                mixed_rows[at, :] = value[:, n * PATCH : (n + 1) * PATCH]
        for n in range(4):
            keep(4 * c + n).start()

    early = 3
    each(early, mix)

    own1.wait()
    all_of(others(rx1, 1), recv_sem.at[0])
    for copy in halos:
        copy.wait_recv()

    window = lax.fori_loop(
        0, devices, lambda s, total: total + rx1[s].astype(F32), jnp.zeros((wrows, PATCH), F32)
    ).astype(BF16)
    height = tile_x + 2 * HALO
    fx = (iota((height, wrows), 0) + (ix * tile_x - HALO)).astype(F32)
    first_x = (4 * (ix * tile_x - 3) - 11 + 26) // 26 - 1
    at_x = (fx + 0.5) * (2.0 / 13.0) - 0.5 + corner[0].astype(F32)
    px = (iota((height, wrows), 1) + (first_x + corner[0])).astype(F32)
    wx = jnp.maximum(0.0, 1.0 - jnp.abs(at_x - px)).astype(BF16)
    lane_y = iota((PATCH, PATCH), 0)
    lane_y = lane_y - jnp.where(lane_y >= PATCH - 16, PATCH, 0)
    fy = (lane_y + iy * tile_y).astype(F32)
    first_y = (4 * (iy * tile_y - 3) - 11 + 26) // 26 - 1
    at_y = (fy + 0.5) * (2.0 / 13.0) - 0.5 + corner[1].astype(F32)
    py = ((iota((PATCH, PATCH), 1) & (WCOLS - 1)) + (first_y + corner[1])).astype(F32)
    wy = jnp.maximum(0.0, 1.0 - jnp.abs(at_y - py))
    group_y = iota((PATCH, PATCH), 1) // WCOLS

    side = lax.dot_general(cols_in[...], place, TN, preferred_element_type=F32)
    side_low = lax.dot_general(corners_in[0], place, TN, preferred_element_type=F32)
    side_high = lax.dot_general(corners_in[1], place, TN, preferred_element_type=F32)

    gi = iota((height, PATCH), 0) + (ix * tile_x - HALO)
    gj = iota((height, PATCH), 1)
    gj = gj - jnp.where(gj >= PATCH - 16, PATCH, 0) + iy * tile_y
    inside = (gi >= 0) & (gi < nx * tile_x) & (gj >= 0) & (gj < ny * tile_y)
    final = []
    for f in range(FIELDS):
        wy_f = jnp.where(group_y == f, wy, 0.0).astype(BF16)
        partial = lax.dot_general(window, wy_f, NT, preferred_element_type=F32).astype(BF16)
        forcing = dot(wx, partial)
        cut = slice(f * PATCH, (f + 1) * PATCH)
        state = jnp.concatenate(
            [
                rows_in[0, f] + side_low[56:64, cut],
                centre[f] + side[0:tile_x, cut],
                rows_in[1, f] + side_high[0:8, cut],
            ],
            axis=0,
        )
        state = jnp.where(inside, state, 0.0)
        for _ in range(STEPS):
            beside = (
                pltpu.roll(state, 1, 0) + pltpu.roll(state, height - 1, 0)
                + pltpu.roll(state, 1, 1) + pltpu.roll(state, PATCH - 1, 1)
            )
            state = state + DIFFUSE * (beside - 4.0 * state) + RELAX * (forcing - state)
            state = jnp.where(inside, state, 0.0)
        state = state[HALO : HALO + tile_x]
        nest[f] = state[:, 0:tile_y]
        final.append(state)

    nest_copy = pltpu.make_async_copy(nest, nest_out, nest_sem)
    nest_copy.start()
    skin_copy.wait()
    flux_tile[:, 0:tile_y] = skin[...]
    heat = flux_tile[...]
    u, v, ta, qa = final
    drag = DRAG * jnp.sqrt(1.0 + u * u + v * v)
    lane = iota((tile_x // 4, PATCH), 1)
    for f, flux in enumerate((drag * (ta - heat), drag * (qa - 0.5 * heat), drag * u, drag * v)):
        flux_tile[...] = flux
        f0, f1, f2, f3 = [flux_tile[pl.ds(n, tile_x // 4, stride=4), :] for n in range(4)]
        f1, f2 = pltpu.roll(f1, 96, 1), pltpu.roll(f2, 64, 1)
        flux_rows[pl.ds(0, blocks // 3, stride=3), :] = jnp.where(lane < 96, f0, f1)
        flux_rows[pl.ds(1, blocks // 3, stride=3), :] = jnp.where(lane < 64, f1, f2)
        flux_rows[pl.ds(2, blocks // 3, stride=3), :] = jnp.where(lane < 32, f2, pltpu.roll(f3, 32, 1))
        flux_pack[f * 256 : f * 256 + blocks, :] = flux_rows[...].astype(BF16)

    def part(ref, device, rows):
        return ref.at[pl.ds(pl.multiple_of(device * rows, 16), rows)]

    def flux_to(other):
        return pltpu.make_async_remote_copy(
            src_ref=part(tx2, other, jp),
            dst_ref=part(rx2, me, jp),
            send_sem=send_sem.at[1],
            recv_sem=recv_sem.at[1],
            device_id=place_of(other),
            device_id_type=MESH,
        )

    turns = devices // per

    def dispatch(c):
        if power:
            turn = ((c + 1) & (turns - 1)) ^ (me >> (per.bit_length() - 1))
        else:
            turn = lax.rem(c + lax.div(me, per), turns)
        rows = pl.ds(pl.multiple_of(turn * chunk, chunk), chunk)
        tx2[rows, :] = dot(pmat[rows, :], flux_pack[...]).astype(BF16)
        for n in range(per):
            other = turn * per + n

            @pl.when(other != me)
            def _():
                flux_to(other).start()

    each(turns, dispatch)
    own2 = pltpu.make_async_copy(part(tx2, me, jp), part(rx2, me, jp), local_sem.at[2])
    own2.start()

    got = rx1[:, 0:16, :].astype(F32)[:, 0, :].astype(BF16)

    def spread_slots(pitch, fields):
        period = math.lcm(pitch, PATCH)
        a, b = iota((PATCH, period), 0) - SLOT_LANE, iota((PATCH, period), 1)
        rank = b - pitch * sum([jnp.where(b >= n * pitch, 1, 0) for n in range(1, period // pitch)])
        inner = sum([jnp.where(rank >= f * cap, 1, 0) for f in range(1, fields + 1)])
        tiled = dot(got, hot((a == rank - inner * cap) & (a >= 0) & (inner < fields)))
        tiled = jnp.where(tiled > 0.5, tiled * 8.0 + inner[0:1].astype(F32), 0.0)
        tiled = jnp.concatenate([tiled] * (devices * pitch // period), axis=1)
        s, l = iota(tiled.shape, 0), iota(tiled.shape, 1)
        mine = (l >= s * pitch) & (l < (s + 1) * pitch)
        return jnp.sum(jnp.where(mine, tiled, 0.0), axis=0, keepdims=True).astype(jnp.int32) - 8

    each(MARINE // 4 - early, lambda c: mix(c + early))
    exchange_copy.wait()
    coarse_rows[...] = jnp.zeros(coarse_rows.shape, F32)
    for g in range(MARINE):
        coarse_rows[g * 8 : g * 8 + FIELDS, :] = exchange[:, g * PATCH : (g + 1) * PATCH]
    amat[...] = hot(iota((MARINE * 8, devices * jp), 0) == spread_slots(jp, FIELDS))
    count = jnp.sum(amat[...].astype(F32), axis=1, keepdims=True)
    qmat[...] = hot(iota((MARINE, devices * rp), 0) * 8 == spread_slots(rp, 1))
    least = jnp.maximum(count, 1.0)
    empty = jnp.where(count == 0.0, coarse_rows[...], 0.0)
    skin_base = mixed_rows[pl.ds(0, MARINE, stride=pitch), :]

    own2.wait()
    all_of(others(rx2, jp), recv_sem.at[1])
    forced[...] = (dot(amat[...], rx2[...]) + empty) / least
    new_skin = skin_base + op[0:1, 0:1] * forced[pl.ds(0, MARINE, stride=8), :]

    def select(matrix, value, dims):
        high = value.astype(BF16)
        low = (value - high.astype(F32)).astype(BF16)
        both = lax.dot_general(
            matrix, jnp.concatenate([high, low], axis=1), dims, preferred_element_type=F32
        )
        return both[:, 0:PATCH] + both[:, PATCH:]

    tx3[...] = select(qmat[...], new_skin, TN).reshape(tx3.shape)
    send(2, lambda other: tx3.at[other, pl.ds(0, cap)], rx3.at[me, pl.ds(0, cap)])
    own3 = pltpu.make_async_copy(tx3.at[me, pl.ds(0, cap)], rx3.at[me, pl.ds(0, cap)], local_sem.at[3])
    own3.start()

    for g in range(MARINE):
        forced_out[:, g * PATCH : (g + 1) * PATCH] = forced[g * 8 : g * 8 + FIELDS, :]
    where_from = hot(iota((blocks, devices * rp), 1) == owner_col * rp + rank_col)
    for copy in halos:
        copy.wait_send()
    all_of(others(tx1, 1), send_sem.at[0])
    all_of(others(tx2, jp), send_sem.at[1])
    own3.wait()
    all_of(rx3.at[pl.ds(0, devices - 1), pl.ds(0, cap)], recv_sem.at[2])
    flux_rows[...] = select(where_from, rx3[...].reshape(devices * rp, PATCH), (((1,), (0,)), ((), ())))
    h0, h1, h2 = [flux_rows[pl.ds(n, blocks // 3, stride=3), :] for n in range(3)]
    h1 = pltpu.roll(h1, 64, 1)
    quarter = tile_x // 4
    flux_tile[pl.ds(0, quarter, stride=4), :] = h0
    flux_tile[pl.ds(1, quarter, stride=4), :] = jnp.where(
        lane < 32, pltpu.roll(h0, 32, 1), pltpu.roll(h1, 96, 1)
    )
    flux_tile[pl.ds(2, quarter, stride=4), :] = jnp.where(lane < 64, h1, pltpu.roll(h2, 64, 1))
    flux_tile[pl.ds(3, quarter, stride=4), :] = pltpu.roll(h2, 96, 1)
    heat_out[...] = flux_tile[:, 0:tile_y]
    nest_copy.wait()
    all_of(tx3.at[pl.ds(0, devices - 1), pl.ds(0, cap)], send_sem.at[2])
    each(MARINE, lambda g: keep(g).wait())


def finish(
    parts,
    nest, mixed, forced, heat, op, nest_out, marine_out, heat_out,
    nest_near, marine_near, forced_near, heat_near, op_near,
    in_sem, out_sem, part_in, part_out,
):
    pairs = [(forced, forced_near), (op, op_near), (nest, nest_near), (heat, heat_near)]
    copies = [pltpu.make_async_copy(far, near, in_sem.at[n]) for n, (far, near) in enumerate(pairs)]
    width = marine_near.shape[3]
    cuts = [pl.ds(n * width, width) for n in range(parts)]
    fetches = [
        pltpu.make_async_copy(mixed.at[:, :, cut], marine_near.at[n], part_in.at[n])
        for n, cut in enumerate(cuts)
    ]
    for copy in copies[:2] + fetches + copies[2:]:
        copy.start()
    copies[0].wait()
    copies[1].wait()
    stores = []
    for n, cut in enumerate(cuts):
        fetches[n].wait()
        push = forced_near[:, cut]
        for layer in range(op.shape[0]):
            marine_near[n, layer] = marine_near[n, layer] + op_near[layer : layer + 1, 0:1] * push
        stores.append(pltpu.make_async_copy(marine_near.at[n], marine_out.at[:, :, cut], part_out.at[n]))
        stores[-1].start()
    for n, (near, far) in enumerate([(nest_near, nest_out), (heat_near, heat_out)]):
        copies[2 + n].wait()
        stores.append(pltpu.make_async_copy(near, far, out_sem.at[n]))
        stores[-1].start()
    for copy in stores:
        copy.wait()


def on_device(nx, ny, fine, skin, coarse, holder, corner, owner, position, exchange, marine, op):
    devices = nx * ny
    tile_x, tile_y = fine.shape[1:]
    blocks = tile_x * tile_y // PATCH
    cap = max(2, (2 * blocks + devices - 1) // devices)
    jp = -(-FIELDS * cap // 16) * 16
    rp = -(-cap // 16) * 16
    spans = [
        first_parent(min((a + 1) * tile_x + 2, nx * tile_x - 1)) - first_parent(a * tile_x - 3) + 2
        for a in range(nx)
    ]
    wrows = -(-max(spans) // 16) * 16
    per = 2 ** int(math.log2(256 // jp))
    last = first_parent((ny - 1) * tile_y - 3) + 1 + 18
    yw = -(-last // PATCH) * PATCH
    layers, cells = marine.shape[1:]
    deep = -(-layers // 16) * 16
    vmem = pl.BlockSpec(memory_space=pltpu.VMEM)
    smem = pl.BlockSpec(memory_space=pltpu.SMEM)
    anywhere = pl.BlockSpec(memory_space=pl.ANY)
    nest, mixed, forced, heat = pl.pallas_call(
        functools.partial(kernel, nx, ny, cap, jp, rp, yw, wrows, per),
        out_shape=(
            jax.ShapeDtypeStruct(fine.shape, F32),
            jax.ShapeDtypeStruct((layers, FIELDS, cells), F32),
            jax.ShapeDtypeStruct((FIELDS, cells), F32),
            jax.ShapeDtypeStruct(skin.shape, F32),
        ),
        in_specs=[smem, smem, vmem, vmem] + [anywhere] * 6,
        out_specs=(anywhere, anywhere, vmem, vmem),
        scratch_shapes=[
            pltpu.VMEM(fine.shape, F32),
            pltpu.VMEM(skin.shape, F32),
            pltpu.VMEM(coarse.shape, BF16),
            pltpu.VMEM(exchange.shape, F32),
            pltpu.VMEM(op.shape, F32),
            pltpu.VMEM(fine.shape, F32),
            pltpu.VMEM((8, 256), jnp.int32),
            pltpu.VMEM((FIELDS, tile_x, PATCH), F32),
            pltpu.VMEM((32, 256), BF16),
            pltpu.VMEM((2, FIELDS, HALO, PATCH), F32),
            pltpu.VMEM((32, 256), BF16),
            pltpu.VMEM((2, 32, PATCH), BF16),
            pltpu.VMEM((devices, wrows, PATCH), BF16),
            pltpu.VMEM((devices, wrows, PATCH), BF16),
            pltpu.VMEM((devices * jp, FIELDS * 256), BF16),
            pltpu.VMEM((tile_x, PATCH), F32),
            pltpu.VMEM((blocks, PATCH), F32),
            pltpu.VMEM((FIELDS * 256, PATCH), BF16),
            pltpu.VMEM((devices * jp, PATCH), BF16),
            pltpu.VMEM((devices * jp, PATCH), BF16),
            pltpu.VMEM((MARINE * 8, devices * jp), BF16),
            pltpu.VMEM((MARINE, devices * rp), BF16),
            pltpu.VMEM((devices, rp, PATCH), F32),
            pltpu.VMEM((devices, rp, PATCH), F32),
            pltpu.VMEM((MARINE, deep, 8, PATCH), F32),
            pltpu.VMEM((MARINE, deep, 8, PATCH), F32),
            pltpu.VMEM((deep, 256), F32),
            pltpu.VMEM((MARINE * 8, PATCH), F32),
            pltpu.VMEM((MARINE * 8, PATCH), F32),
            pltpu.SemaphoreType.DMA((5,)),
            pltpu.SemaphoreType.DMA((MARINE,)),
            pltpu.SemaphoreType.DMA((MARINE,)),
            pltpu.SemaphoreType.DMA,
            pltpu.SemaphoreType.DMA((4,)),
            pltpu.SemaphoreType.DMA((8,)),
            pltpu.SemaphoreType.DMA((8,)),
            pltpu.SemaphoreType.DMA((3,)),
            pltpu.SemaphoreType.DMA((3,)),
        ],
        compiler_params=pltpu.CompilerParams(
            collective_id=0, has_side_effects=True, vmem_limit_bytes=56 * 1024 * 1024
        ),
    )(
        holder, corner, owner.reshape(1, blocks), position.reshape(1, blocks),
        fine, skin, coarse, exchange, jnp.transpose(marine, (1, 0, 2)), op,
    )
    parts = 8
    nest, marine_new, heat = pl.pallas_call(
        functools.partial(finish, parts),
        out_shape=(
            jax.ShapeDtypeStruct(fine.shape, F32),
            jax.ShapeDtypeStruct((layers, FIELDS, cells), F32),
            jax.ShapeDtypeStruct(skin.shape, F32),
        ),
        in_specs=[anywhere] * 5,
        out_specs=(anywhere,) * 3,
        scratch_shapes=[
            pltpu.VMEM(fine.shape, F32),
            pltpu.VMEM((parts, layers, FIELDS, cells // parts), F32),
            pltpu.VMEM((FIELDS, cells), F32),
            pltpu.VMEM(skin.shape, F32),
            pltpu.VMEM(op.shape, F32),
            pltpu.SemaphoreType.DMA((4,)),
            pltpu.SemaphoreType.DMA((2,)),
            pltpu.SemaphoreType.DMA((parts,)),
            pltpu.SemaphoreType.DMA((parts,)),
        ],
        compiler_params=pltpu.CompilerParams(vmem_limit_bytes=56 * 1024 * 1024),
    )(nest, mixed, forced, heat, op)
    return nest, jnp.transpose(marine_new, (1, 0, 2)), heat


def solution(mesh):
    in_specs = (
        P(None, "gx", "gy"),
        P("gx", "gy"),
        P(None, "gx", "gy"),
        P(),
        P(),
        P(("gx", "gy"), None),
        P(("gx", "gy")),
        P(None, ("gx", "gy")),
        P(None, None, ("gx", "gy")),
        P(),
    )
    out_specs = (P(None, "gx", "gy"), P(None, None, ("gx", "gy")), P("gx", "gy"))
    return jax.shard_map(
        functools.partial(on_device, mesh.shape["gx"], mesh.shape["gy"]),
        mesh=mesh,
        in_specs=in_specs,
        out_specs=out_specs,
        check_vma=False,
    )
```

```python
import functools
import math

import jax
import jax.numpy as jnp
from jax import lax
from jax.experimental import pallas as pl
from jax.experimental.pallas import tpu as pltpu
from jax.sharding import PartitionSpec as P

FIELDS = 4
PATCH = 128
MARINE = 32
STEPS = 4
WCOLS = 32
SLOT_LANE = 18
HALO = 8
DIFFUSE = 0.24
RELAX = 0.3
DRAG = 0.5
F32 = jnp.float32
BF16 = jnp.bfloat16
MESH = pl.DeviceIdType.MESH
NT = (((1,), (1,)), ((), ()))
TN = (((0,), (0,)), ((), ()))


def iota(shape, dim):
    return lax.broadcasted_iota(jnp.int32, shape, dim)


def hot(condition):
    return jnp.where(condition, 1.0, 0.0).astype(BF16)


def dot(a, b):
    return jnp.dot(a, b, preferred_element_type=F32)


def first_parent(first_fine):
    return (4 * first_fine - 11) // 26


def kernel(
    nx, ny, cap, jp, rp, yw, wrows, per,
    holder, corner, owner, position, fine_far, skin_far, coarse_far, exchange_far, marine, op_far,
    nest_out, marine_out, forced_out, heat_out,
    fine, skin, coarse, exchange, op, nest, index_row, centre, strips, rows_in, cols_in, corners_in,
    tx1, rx1, pmat, flux_tile, flux_rows, flux_pack, tx2, rx2, amat, qmat, tx3, rx3,
    marine_in, mixed, op_pad, coarse_rows, forced,
    in_sem, marine_sem, out_sem, nest_sem, local_sem, halo_send, halo_recv, send_sem, recv_sem,
):
    tile_x, tile_y = fine.shape[1], fine.shape[2]
    blocks = owner.shape[1]
    layers = op.shape[0]
    devices = nx * ny
    ix, iy = lax.axis_index("gx"), lax.axis_index("gy")
    me = ix * ny + iy

    arrays = [(coarse_far, coarse), (fine_far, fine), (skin_far, skin), (exchange_far, exchange), (op_far, op)]
    arrays = [pltpu.make_async_copy(far, near, in_sem.at[n]) for n, (far, near) in enumerate(arrays)]
    for copy in arrays:
        copy.start()
    coarse_copy, fine_copy, skin_copy, exchange_copy, op_copy = arrays

    def each(count, work):
        def one(n, carry):
            work(n)
            return carry

        lax.fori_loop(0, count, one, 0)

    power = devices & (devices - 1) == 0 and ny & (ny - 1) == 0 and devices >= 8

    def place_of(device):
        if power:
            return (device >> (ny.bit_length() - 1), device & (ny - 1))
        return (lax.div(device, ny), lax.rem(device, ny))

    def to_others(work):
        if not power:
            each(devices - 1, lambda n: work(lax.rem(me + 1 + n, devices)))
            return

        def nth(n):
            return (me + n) & (devices - 1)

        each(devices - 1, lambda n: work(nth(n + 1)))

    rx3[...] = jnp.zeros(rx3.shape, F32)
    barrier = pltpu.get_barrier_semaphore()
    to_others(
        lambda other: pl.semaphore_signal(
            barrier, inc=1, device_id=place_of(other), device_id_type=MESH
        )
    )
    def ocean_block(ref, g):
        return ref.at[:, :, pl.ds(pl.multiple_of(g * PATCH, PATCH), PATCH)]

    def fetch(g):
        return pltpu.make_async_copy(
            ocean_block(marine, g), marine_in.at[g, pl.ds(0, layers), pl.ds(0, FIELDS), :], marine_sem.at[g]
        )

    def keep(g):
        return pltpu.make_async_copy(
            mixed.at[g, pl.ds(0, layers), pl.ds(0, FIELDS), :], ocean_block(marine_out, g), out_sem.at[g]
        )

    each(MARINE, lambda g: fetch(g).start())

    fine_copy.wait()
    for f in range(FIELDS):
        centre[f, :, :] = jnp.zeros((tile_x, PATCH), F32)
        centre[f, :, 0:tile_y] = fine[f]
    wide = jnp.concatenate([centre[f].astype(BF16) for f in range(FIELDS)], axis=1)
    r = iota((32, FIELDS * PATCH), 0)
    field_col = ((r & 15) >> 2) * PATCH + (r & 3)
    lane = iota((32, FIELDS * PATCH), 1)
    pick = hot(lane == field_col + jnp.where(r >= 16, tile_y - 4, 0))
    place = hot(lane == field_col + jnp.where(r >= 16, tile_y, PATCH - 4))
    wide = jnp.concatenate([wide, jnp.zeros((256 - tile_x, FIELDS * PATCH), BF16)], axis=0)
    strips[...] = lax.dot_general(pick, wide, NT, preferred_element_type=F32).astype(BF16)

    index_row[...] = jnp.full(index_row.shape, -1, jnp.int32)
    index_row[0:1, 0:blocks] = owner[...]
    index_row[1:2, 0:blocks] = position[...]
    owner_row, pos_row = index_row[0:1, :], index_row[1:2, :]
    k0, k1 = iota((blocks, 256), 0), iota((blocks, 256), 1)
    owner_col = jnp.sum(
        jnp.where(k0 == k1, owner_row.astype(F32), 0.0), axis=1, keepdims=True
    ).astype(jnp.int32)
    same = owner_col == owner_row
    rank_row = jnp.sum(jnp.where(same & (k0 < k1), 1.0, 0.0), axis=0, keepdims=True).astype(jnp.int32)
    rank_col = jnp.sum(jnp.where(same & (k1 < k0), 1.0, 0.0), axis=1, keepdims=True).astype(jnp.int32)

    owners_hot = jnp.where(iota((devices, 256), 0) == owner_row, 1.0, 0.0)
    weighted = (owners_hot * (pos_row + 1).astype(F32)).astype(BF16)
    ranks_hot = hot(iota((PATCH, 256), 0) - SLOT_LANE == rank_row)
    slots = lax.dot_general(weighted, ranks_hot, NT, preferred_element_type=F32)

    coarse_copy.wait()
    cells = coarse.shape[1]
    away = (holder[0] - me) * 65536
    q = iota((cells, yw), 0)
    choose_y = hot(q == iota((cells, yw), 1) + (corner[1] - 1))
    p = iota((wrows, cells), 1) - iota((wrows, cells), 0) - (corner[0] + away)
    choose_x = jnp.concatenate([hot(p == first_parent(a * tile_x - 3)) for a in range(nx)], axis=0)
    windows = []
    for f in range(FIELDS):
        narrow = dot(coarse[f], choose_y).astype(BF16)
        windows.append(dot(choose_x, narrow))
    lane_group = iota((nx * wrows, PATCH), 1) // WCOLS
    lane = iota((wrows, PATCH), 1)
    slot_place = (iota((wrows, PATCH), 0) == 0) & (lane >= SLOT_LANE) & (lane < WCOLS)
    for b in range(ny):
        base = first_parent(b * tile_y - 3) + 1
        piece = jnp.zeros((nx * wrows, PATCH), F32)
        for f in range(FIELDS):
            moved = pltpu.roll(windows[f], (f * WCOLS - base) % yw, 1)[:, 0:PATCH]
            piece = jnp.where(lane_group == f, moved, piece)
        for a in range(nx):
            d = a * ny + b
            part = piece[a * wrows : (a + 1) * wrows]
            tx1[d] = jnp.where(slot_place, slots[d : d + 1, :], part).astype(BF16)

    pl.semaphore_wait(barrier, devices - 1)

    def send(phase, source, target):
        to_others(
            lambda other: pltpu.make_async_remote_copy(
                src_ref=source(other),
                dst_ref=target,
                send_sem=send_sem.at[phase],
                recv_sem=recv_sem.at[phase],
                device_id=place_of(other),
                device_id_type=MESH,
            ).start()
        )

    def all_of(ref, sem):
        pltpu.make_async_copy(ref, ref, sem).wait()

    def others(ref, rows):
        return ref.at[pl.ds(0, (devices - 1) * rows)]

    west, east = lax.rem(ix + nx - 1, nx), lax.rem(ix + 1, nx)
    south, north = lax.rem(iy + ny - 1, ny), lax.rem(iy + 1, ny)
    left, right = pl.ds(0, 16), pl.ds(16, 16)
    low, high = pl.ds(0, 128), pl.ds(128, 128)
    halos = [
        (centre.at[:, pl.ds(tile_x - HALO, HALO), :], rows_in.at[0], (east, iy)),
        (centre.at[:, pl.ds(0, HALO), :], rows_in.at[1], (west, iy)),
        (strips.at[right], cols_in.at[left], (ix, north)),
        (strips.at[left], cols_in.at[right], (ix, south)),
        (strips.at[right, high], corners_in.at[0, left], (east, north)),
        (strips.at[left, high], corners_in.at[0, right], (east, south)),
        (strips.at[right, low], corners_in.at[1, left], (west, north)),
        (strips.at[left, low], corners_in.at[1, right], (west, south)),
    ]
    halos = [
        pltpu.make_async_remote_copy(
            src_ref=src, dst_ref=dst, send_sem=halo_send.at[n], recv_sem=halo_recv.at[n],
            device_id=where, device_id_type=MESH,
        )
        for n, (src, dst, where) in enumerate(halos)
    ]
    for copy in halos:
        copy.start()
    send(0, lambda other: tx1.at[other], rx1.at[me])
    own1 = pltpu.make_async_copy(tx1.at[me], rx1.at[me], local_sem.at[1])
    own1.start()

    target = owner_row * jp + rank_row

    chunk = per * jp

    def dispatch_rows(c):
        start = pl.multiple_of(c * chunk, chunk)
        row = iota((chunk, 256), 0) + start
        for f in range(FIELDS):
            pmat[pl.ds(start, chunk), f * 256 : (f + 1) * 256] = hot(row == target + f * cap)

    each(devices // per, dispatch_rows)
    flux_pack[...] = jnp.zeros(flux_pack.shape, BF16)

    deep = marine_in.shape[1]
    op_copy.wait()
    op_pad[...] = jnp.zeros(op_pad.shape, F32)
    op_pad[0:layers, 0:layers] = op[...]
    op_high = op_pad[...].astype(BF16).astype(F32)
    op_low = op_pad[...] - op_high
    op_three = op_high + pltpu.roll(op_high, deep, 1) + pltpu.roll(op_low, 2 * deep, 1)
    op_three = op_three.astype(BF16)[:, 0 : 3 * deep]
    pitch = deep * 8
    marine_in[:, layers:, :, :] = jnp.zeros((MARINE, deep - layers, 8, PATCH), F32)
    marine_rows = marine_in.reshape(MARINE * pitch, PATCH)
    mixed_rows = mixed.reshape(MARINE * pitch, PATCH)

    def mix(c):
        for n in range(4):
            fetch(4 * c + n).wait()
        for f in range(FIELDS):
            rows = [pl.ds((4 * c + n) * pitch + f, deep, stride=8) for n in range(4)]
            value = jnp.concatenate([marine_rows[at, :] for at in rows], axis=1)
            m_high = value.astype(BF16)
            m_low = (value - m_high.astype(F32)).astype(BF16)
            value = dot(op_three, jnp.concatenate([m_high, m_low, m_high], axis=0))
            for n, at in enumerate(rows):
                mixed_rows[at, :] = value[:, n * PATCH : (n + 1) * PATCH]
        for n in range(4):
            keep(4 * c + n).start()

    early = 3
    each(early, mix)

    own1.wait()
    all_of(others(rx1, 1), recv_sem.at[0])
    for copy in halos:
        copy.wait_recv()

    window = lax.fori_loop(
        0, devices, lambda s, total: total + rx1[s].astype(F32), jnp.zeros((wrows, PATCH), F32)
    ).astype(BF16)
    height = tile_x + 2 * HALO
    fx = (iota((height, wrows), 0) + (ix * tile_x - HALO)).astype(F32)
    first_x = (4 * (ix * tile_x - 3) - 11 + 26) // 26 - 1
    at_x = (fx + 0.5) * (2.0 / 13.0) - 0.5 + corner[0].astype(F32)
    px = (iota((height, wrows), 1) + (first_x + corner[0])).astype(F32)
    wx = jnp.maximum(0.0, 1.0 - jnp.abs(at_x - px)).astype(BF16)
    lane_y = iota((PATCH, PATCH), 0)
    lane_y = lane_y - jnp.where(lane_y >= PATCH - 16, PATCH, 0)
    fy = (lane_y + iy * tile_y).astype(F32)
    first_y = (4 * (iy * tile_y - 3) - 11 + 26) // 26 - 1
    at_y = (fy + 0.5) * (2.0 / 13.0) - 0.5 + corner[1].astype(F32)
    py = ((iota((PATCH, PATCH), 1) & (WCOLS - 1)) + (first_y + corner[1])).astype(F32)
    wy = jnp.maximum(0.0, 1.0 - jnp.abs(at_y - py))
    group_y = iota((PATCH, PATCH), 1) // WCOLS

    side = lax.dot_general(cols_in[...], place, TN, preferred_element_type=F32)
    side_low = lax.dot_general(corners_in[0], place, TN, preferred_element_type=F32)
    side_high = lax.dot_general(corners_in[1], place, TN, preferred_element_type=F32)

    gi = iota((height, PATCH), 0) + (ix * tile_x - HALO)
    gj = iota((height, PATCH), 1)
    gj = gj - jnp.where(gj >= PATCH - 16, PATCH, 0) + iy * tile_y
    inside = (gi >= 0) & (gi < nx * tile_x) & (gj >= 0) & (gj < ny * tile_y)
    final = []
    for f in range(FIELDS):
        wy_f = jnp.where(group_y == f, wy, 0.0).astype(BF16)
        partial = lax.dot_general(window, wy_f, NT, preferred_element_type=F32).astype(BF16)
        forcing = dot(wx, partial)
        cut = slice(f * PATCH, (f + 1) * PATCH)
        state = jnp.concatenate(
            [
                rows_in[0, f] + side_low[56:64, cut],
                centre[f] + side[0:tile_x, cut],
                rows_in[1, f] + side_high[0:8, cut],
            ],
            axis=0,
        )
        state = jnp.where(inside, state, 0.0)
        for _ in range(STEPS):
            beside = (
                pltpu.roll(state, 1, 0) + pltpu.roll(state, height - 1, 0)
                + pltpu.roll(state, 1, 1) + pltpu.roll(state, PATCH - 1, 1)
            )
            state = state + DIFFUSE * (beside - 4.0 * state) + RELAX * (forcing - state)
            state = jnp.where(inside, state, 0.0)
        state = state[HALO : HALO + tile_x]
        nest[f] = state[:, 0:tile_y]
        final.append(state)

    nest_copy = pltpu.make_async_copy(nest, nest_out, nest_sem)
    nest_copy.start()
    skin_copy.wait()
    flux_tile[:, 0:tile_y] = skin[...]
    heat = flux_tile[...]
    u, v, ta, qa = final
    drag = DRAG * jnp.sqrt(1.0 + u * u + v * v)
    lane = iota((tile_x // 4, PATCH), 1)
    for f, flux in enumerate((drag * (ta - heat), drag * (qa - 0.5 * heat), drag * u, drag * v)):
        flux_tile[...] = flux
        f0, f1, f2, f3 = [flux_tile[pl.ds(n, tile_x // 4, stride=4), :] for n in range(4)]
        f1, f2 = pltpu.roll(f1, 96, 1), pltpu.roll(f2, 64, 1)
        flux_rows[pl.ds(0, blocks // 3, stride=3), :] = jnp.where(lane < 96, f0, f1)
        flux_rows[pl.ds(1, blocks // 3, stride=3), :] = jnp.where(lane < 64, f1, f2)
        flux_rows[pl.ds(2, blocks // 3, stride=3), :] = jnp.where(lane < 32, f2, pltpu.roll(f3, 32, 1))
        flux_pack[f * 256 : f * 256 + blocks, :] = flux_rows[...].astype(BF16)

    def part(ref, device, rows):
        return ref.at[pl.ds(pl.multiple_of(device * rows, 16), rows)]

    def flux_to(other):
        return pltpu.make_async_remote_copy(
            src_ref=part(tx2, other, jp),
            dst_ref=part(rx2, me, jp),
            send_sem=send_sem.at[1],
            recv_sem=recv_sem.at[1],
            device_id=place_of(other),
            device_id_type=MESH,
        )

    turns = devices // per

    def dispatch(c):
        if power:
            turn = (c + 1 + (me >> (per.bit_length() - 1))) & (turns - 1)
        else:
            turn = lax.rem(c + lax.div(me, per), turns)
        rows = pl.ds(pl.multiple_of(turn * chunk, chunk), chunk)
        tx2[rows, :] = dot(pmat[rows, :], flux_pack[...]).astype(BF16)
        for n in range(per):
            other = turn * per + n

            @pl.when(other != me)
            def _():
                flux_to(other).start()

    each(turns, dispatch)
    own2 = pltpu.make_async_copy(part(tx2, me, jp), part(rx2, me, jp), local_sem.at[2])
    own2.start()

    got = rx1[:, 0:16, :].astype(F32)[:, 0, :].astype(BF16)

    def spread_slots(pitch, fields):
        period = math.lcm(pitch, PATCH)
        a, b = iota((PATCH, period), 0) - SLOT_LANE, iota((PATCH, period), 1)
        rank = b - pitch * sum([jnp.where(b >= n * pitch, 1, 0) for n in range(1, period // pitch)])
        inner = sum([jnp.where(rank >= f * cap, 1, 0) for f in range(1, fields + 1)])
        tiled = dot(got, hot((a == rank - inner * cap) & (a >= 0) & (inner < fields)))
        tiled = jnp.where(tiled > 0.5, tiled * 8.0 + inner[0:1].astype(F32), 0.0)
        tiled = jnp.concatenate([tiled] * (devices * pitch // period), axis=1)
        s, l = iota(tiled.shape, 0), iota(tiled.shape, 1)
        mine = (l >= s * pitch) & (l < (s + 1) * pitch)
        return jnp.sum(jnp.where(mine, tiled, 0.0), axis=0, keepdims=True).astype(jnp.int32) - 8

    each(MARINE // 4 - early, lambda c: mix(c + early))
    exchange_copy.wait()
    coarse_rows[...] = jnp.zeros(coarse_rows.shape, F32)
    for g in range(MARINE):
        coarse_rows[g * 8 : g * 8 + FIELDS, :] = exchange[:, g * PATCH : (g + 1) * PATCH]
    amat[...] = hot(iota((MARINE * 8, devices * jp), 0) == spread_slots(jp, FIELDS))
    count = jnp.sum(amat[...].astype(F32), axis=1, keepdims=True)
    qmat[...] = hot(iota((MARINE, devices * rp), 0) * 8 == spread_slots(rp, 1))
    least = jnp.maximum(count, 1.0)
    empty = jnp.where(count == 0.0, coarse_rows[...], 0.0)
    skin_base = mixed_rows[pl.ds(0, MARINE, stride=pitch), :]

    own2.wait()
    all_of(others(rx2, jp), recv_sem.at[1])
    forced[...] = (dot(amat[...], rx2[...]) + empty) / least
    new_skin = skin_base + op[0:1, 0:1] * forced[pl.ds(0, MARINE, stride=8), :]

    def select(matrix, value, dims):
        high = value.astype(BF16)
        low = (value - high.astype(F32)).astype(BF16)
        both = lax.dot_general(
            matrix, jnp.concatenate([high, low], axis=1), dims, preferred_element_type=F32
        )
        return both[:, 0:PATCH] + both[:, PATCH:]

    tx3[...] = select(qmat[...], new_skin, TN).reshape(tx3.shape)
    send(2, lambda other: tx3.at[other, pl.ds(0, cap)], rx3.at[me, pl.ds(0, cap)])
    own3 = pltpu.make_async_copy(tx3.at[me, pl.ds(0, cap)], rx3.at[me, pl.ds(0, cap)], local_sem.at[3])
    own3.start()

    for g in range(MARINE):
        forced_out[:, g * PATCH : (g + 1) * PATCH] = forced[g * 8 : g * 8 + FIELDS, :]
    where_from = hot(iota((blocks, devices * rp), 1) == owner_col * rp + rank_col)
    for copy in halos:
        copy.wait_send()
    all_of(others(tx1, 1), send_sem.at[0])
    all_of(others(tx2, jp), send_sem.at[1])
    own3.wait()
    all_of(rx3.at[pl.ds(0, devices - 1), pl.ds(0, cap)], recv_sem.at[2])
    flux_rows[...] = select(where_from, rx3[...].reshape(devices * rp, PATCH), (((1,), (0,)), ((), ())))
    h0, h1, h2 = [flux_rows[pl.ds(n, blocks // 3, stride=3), :] for n in range(3)]
    h1 = pltpu.roll(h1, 64, 1)
    quarter = tile_x // 4
    flux_tile[pl.ds(0, quarter, stride=4), :] = h0
    flux_tile[pl.ds(1, quarter, stride=4), :] = jnp.where(
        lane < 32, pltpu.roll(h0, 32, 1), pltpu.roll(h1, 96, 1)
    )
    flux_tile[pl.ds(2, quarter, stride=4), :] = jnp.where(lane < 64, h1, pltpu.roll(h2, 64, 1))
    flux_tile[pl.ds(3, quarter, stride=4), :] = pltpu.roll(h2, 96, 1)
    heat_out[...] = flux_tile[:, 0:tile_y]
    nest_copy.wait()
    all_of(tx3.at[pl.ds(0, devices - 1), pl.ds(0, cap)], send_sem.at[2])
    each(MARINE, lambda g: keep(g).wait())


def finish(
    parts,
    nest, mixed, forced, heat, op, nest_out, marine_out, heat_out,
    nest_near, marine_near, forced_near, heat_near, op_near,
    in_sem, out_sem, part_in, part_out,
):
    pairs = [(forced, forced_near), (op, op_near), (nest, nest_near), (heat, heat_near)]
    copies = [pltpu.make_async_copy(far, near, in_sem.at[n]) for n, (far, near) in enumerate(pairs)]
    width = marine_near.shape[3]
    cuts = [pl.ds(n * width, width) for n in range(parts)]
    fetches = [
        pltpu.make_async_copy(mixed.at[:, :, cut], marine_near.at[n], part_in.at[n])
        for n, cut in enumerate(cuts)
    ]
    for copy in copies[:2] + fetches + copies[2:]:
        copy.start()
    copies[0].wait()
    copies[1].wait()
    stores = []
    for n, cut in enumerate(cuts):
        fetches[n].wait()
        push = forced_near[:, cut]
        for layer in range(op.shape[0]):
            marine_near[n, layer] = marine_near[n, layer] + op_near[layer : layer + 1, 0:1] * push
        stores.append(pltpu.make_async_copy(marine_near.at[n], marine_out.at[:, :, cut], part_out.at[n]))
        stores[-1].start()
    for n, (near, far) in enumerate([(nest_near, nest_out), (heat_near, heat_out)]):
        copies[2 + n].wait()
        stores.append(pltpu.make_async_copy(near, far, out_sem.at[n]))
        stores[-1].start()
    for copy in stores:
        copy.wait()


def on_device(nx, ny, fine, skin, coarse, holder, corner, owner, position, exchange, marine, op):
    devices = nx * ny
    tile_x, tile_y = fine.shape[1:]
    blocks = tile_x * tile_y // PATCH
    cap = max(2, (2 * blocks + devices - 1) // devices)
    jp = -(-FIELDS * cap // 16) * 16
    rp = -(-cap // 16) * 16
    spans = [
        first_parent(min((a + 1) * tile_x + 2, nx * tile_x - 1)) - first_parent(a * tile_x - 3) + 2
        for a in range(nx)
    ]
    wrows = -(-max(spans) // 16) * 16
    per = 2 ** int(math.log2(256 // jp))
    last = first_parent((ny - 1) * tile_y - 3) + 1 + 18
    yw = -(-last // PATCH) * PATCH
    layers, cells = marine.shape[1:]
    deep = -(-layers // 16) * 16
    vmem = pl.BlockSpec(memory_space=pltpu.VMEM)
    smem = pl.BlockSpec(memory_space=pltpu.SMEM)
    anywhere = pl.BlockSpec(memory_space=pl.ANY)
    nest, mixed, forced, heat = pl.pallas_call(
        functools.partial(kernel, nx, ny, cap, jp, rp, yw, wrows, per),
        out_shape=(
            jax.ShapeDtypeStruct(fine.shape, F32),
            jax.ShapeDtypeStruct((layers, FIELDS, cells), F32),
            jax.ShapeDtypeStruct((FIELDS, cells), F32),
            jax.ShapeDtypeStruct(skin.shape, F32),
        ),
        in_specs=[smem, smem, vmem, vmem] + [anywhere] * 6,
        out_specs=(anywhere, anywhere, vmem, vmem),
        scratch_shapes=[
            pltpu.VMEM(fine.shape, F32),
            pltpu.VMEM(skin.shape, F32),
            pltpu.VMEM(coarse.shape, BF16),
            pltpu.VMEM(exchange.shape, F32),
            pltpu.VMEM(op.shape, F32),
            pltpu.VMEM(fine.shape, F32),
            pltpu.VMEM((8, 256), jnp.int32),
            pltpu.VMEM((FIELDS, tile_x, PATCH), F32),
            pltpu.VMEM((32, 256), BF16),
            pltpu.VMEM((2, FIELDS, HALO, PATCH), F32),
            pltpu.VMEM((32, 256), BF16),
            pltpu.VMEM((2, 32, PATCH), BF16),
            pltpu.VMEM((devices, wrows, PATCH), BF16),
            pltpu.VMEM((devices, wrows, PATCH), BF16),
            pltpu.VMEM((devices * jp, FIELDS * 256), BF16),
            pltpu.VMEM((tile_x, PATCH), F32),
            pltpu.VMEM((blocks, PATCH), F32),
            pltpu.VMEM((FIELDS * 256, PATCH), BF16),
            pltpu.VMEM((devices * jp, PATCH), BF16),
            pltpu.VMEM((devices * jp, PATCH), BF16),
            pltpu.VMEM((MARINE * 8, devices * jp), BF16),
            pltpu.VMEM((MARINE, devices * rp), BF16),
            pltpu.VMEM((devices, rp, PATCH), F32),
            pltpu.VMEM((devices, rp, PATCH), F32),
            pltpu.VMEM((MARINE, deep, 8, PATCH), F32),
            pltpu.VMEM((MARINE, deep, 8, PATCH), F32),
            pltpu.VMEM((deep, 256), F32),
            pltpu.VMEM((MARINE * 8, PATCH), F32),
            pltpu.VMEM((MARINE * 8, PATCH), F32),
            pltpu.SemaphoreType.DMA((5,)),
            pltpu.SemaphoreType.DMA((MARINE,)),
            pltpu.SemaphoreType.DMA((MARINE,)),
            pltpu.SemaphoreType.DMA,
            pltpu.SemaphoreType.DMA((4,)),
            pltpu.SemaphoreType.DMA((8,)),
            pltpu.SemaphoreType.DMA((8,)),
            pltpu.SemaphoreType.DMA((3,)),
            pltpu.SemaphoreType.DMA((3,)),
        ],
        compiler_params=pltpu.CompilerParams(
            collective_id=0, has_side_effects=True, vmem_limit_bytes=56 * 1024 * 1024
        ),
    )(
        holder, corner, owner.reshape(1, blocks), position.reshape(1, blocks),
        fine, skin, coarse, exchange, jnp.transpose(marine, (1, 0, 2)), op,
    )
    parts = 8
    nest, marine_new, heat = pl.pallas_call(
        functools.partial(finish, parts),
        out_shape=(
            jax.ShapeDtypeStruct(fine.shape, F32),
            jax.ShapeDtypeStruct((layers, FIELDS, cells), F32),
            jax.ShapeDtypeStruct(skin.shape, F32),
        ),
        in_specs=[anywhere] * 5,
        out_specs=(anywhere,) * 3,
        scratch_shapes=[
            pltpu.VMEM(fine.shape, F32),
            pltpu.VMEM((parts, layers, FIELDS, cells // parts), F32),
            pltpu.VMEM((FIELDS, cells), F32),
            pltpu.VMEM(skin.shape, F32),
            pltpu.VMEM(op.shape, F32),
            pltpu.SemaphoreType.DMA((4,)),
            pltpu.SemaphoreType.DMA((2,)),
            pltpu.SemaphoreType.DMA((parts,)),
            pltpu.SemaphoreType.DMA((parts,)),
        ],
        compiler_params=pltpu.CompilerParams(vmem_limit_bytes=56 * 1024 * 1024),
    )(nest, mixed, forced, heat, op)
    return nest, jnp.transpose(marine_new, (1, 0, 2)), heat


def solution(mesh):
    in_specs = (
        P(None, "gx", "gy"),
        P("gx", "gy"),
        P(None, "gx", "gy"),
        P(),
        P(),
        P(("gx", "gy"), None),
        P(("gx", "gy")),
        P(None, ("gx", "gy")),
        P(None, None, ("gx", "gy")),
        P(),
    )
    out_specs = (P(None, "gx", "gy"), P(None, None, ("gx", "gy")), P("gx", "gy"))
    return jax.shard_map(
        functools.partial(on_device, mesh.shape["gx"], mesh.shape["gy"]),
        mesh=mesh,
        in_specs=in_specs,
        out_specs=out_specs,
        check_vma=False,
    )
```
